32 devices in a mesh: group: 8 (over y, x, core), shuf: 4 (over z).
Axes of the slice: x: 2, y: 2, z: 4, core: 2. Of those that a mesh axis runs over, the one named last changes fastest.
Arguments:
- inputs: bfloat16 [8, 1024, 512], P('group', 'shuf'), may hold values from -8 to 8
- cotangent: bfloat16 [8, 1024, 512], P('group', 'shuf'), may hold values from -8 to 8
- w_uvqk: bfloat16 [512, 2048], P('group'), may hold values from -0.25 to 0.25
- w_out: bfloat16 [512, 512], P('group'), may hold values from -0.25 to 0.25
- send_perm: int32 [8, 4, 32], P('group', 'shuf'), may hold values from 0 to 31, each once within a row
- recv_perm: int32 [8, 4, 32], P('group', 'shuf'), may hold values from 0 to 31, each once within a row
- lengths: int32 [8, 4, 8], P('group', 'shuf'), may hold values from 1 to 128, 256 in all within a row
- prefixes: int32 [8, 4, 8], P('group', 'shuf'), may hold values from 0 to 32
Outputs:
- layer_out: bfloat16 [8, 1024, 512], P('group', 'shuf')
- grad_input: bfloat16 [8, 1024, 512], P('group', 'shuf')
- grad_uvqk: float32 [512, 2048], P('group')
- grad_wout: float32 [512, 512], P('group')
The draws below stay inside these ranges and needn't reach their ends.
All inputs are finite; a program needn't handle non-finite values.
Results may differ from the reference program's by a relative error of at most 0.03.
Values may be sent and summed in bfloat16 or wider, within the bound.
No kernel may reach another device: no remote copies, remote signals or barrier semaphores. Data moves between devices by JAX's collectives and lax.ppermute only.
A program may use at most 64 MiB of HBM per device.

```python
import math
from functools import partial
import jax
import jax.numpy as jnp
import numpy as np
from jax import lax

D = 512
HEADS = 8
ROWS = 256
BLOCK = 8
USERS = 8
BLK_DEV = 32
CAP = 8
MAX_LEN = 128
N_GROUP = 8
N_SHUF = 4


def set_ends(array, rng, least, top_value):
    longest = array.shape.index(max(array.shape))
    spots = []
    for shift in (0, 1):
        where = [jax.random.randint(jax.random.fold_in(rng, axis), (), 0, length) for axis, length in enumerate(array.shape)]
        where[longest] = (where[longest] + shift) % array.shape[longest]
        spots.append(tuple(where))
    return array.at[spots[0]].set(least).at[spots[1]].set(top_value)


def with_spikes(values, key, source, target, parts, factor):
    def block_of(axis_at):
        return (jnp.arange(values.shape[axis_at]) // (values.shape[axis_at] // parts)).reshape((-1,) + (1,) * (values.ndim - 1 - axis_at))

    first = jax.random.permutation(key, parts)[block_of(target)]
    other_side = (block_of(target) + parts // 2) % parts
    return jnp.where((block_of(source) == first) | (block_of(source) == other_side), factor * values, values)


def steps_of(key, dims, shards, smallest, largest):
    def one(dim, shards_of):
        heights = jax.random.uniform(jax.random.fold_in(jax.random.fold_in(key, 6), dim), (shards_of,), jnp.float32, smallest / len(shards), largest / len(shards))
        return jnp.repeat(jnp.exp(heights), dims[dim] // shards_of).reshape((-1,) + (1,) * (len(dims) - dim - 1))

    gain = one(*shards[0])
    for cut in shards[1:]:
        gain = gain * one(*cut)
    return gain


def split_up(number_of, total, limit, lean):
    portions = [(1 << 20) // math.isqrt(rank ** lean) + 1 for rank in range(2, number_of + 1)]
    surplus, holding = total - limit - (number_of - 1), [1] * (number_of - 1)
    while surplus > 0:
        movable = [i for i in range(number_of - 1) if holding[i] < limit]
        whole, remaining = sum([portions[i] for i in movable]), surplus
        for i in movable:
            more = min(limit - holding[i], max(1, remaining * portions[i] // whole), surplus)
            holding[i] = holding[i] + more
            surplus = surplus - more
    return np.array([limit] + holding)


def ragged_sizes(own_key, count, total, bound, lean):
    if count == 2:
        one = jax.random.randint(own_key, (), max(1, total - bound), min(bound, total - 1) + 1)
        return jnp.stack([one, total - one])
    sizes = jnp.asarray(split_up(count, total, bound, lean), jnp.int32)
    pairs = (count - 1) // 2
    giver, receiver = sizes[1:1 + 2 * pairs:2], sizes[2:2 + 2 * pairs:2]
    slack = jnp.minimum(giver - 1, bound - receiver)
    shifted = jax.random.randint(jax.random.fold_in(own_key, 1), (pairs,), 0, 1 << 20) % (slack + 1)
    sizes = sizes.at[1:1 + 2 * pairs:2].set(giver - shifted).at[2:2 + 2 * pairs:2].set(receiver + shifted)
    return sizes[jax.random.permutation(jax.random.fold_in(own_key, 2), count)]


def noise(stream_key, shape, spread, bound, split=(), kind=jnp.bfloat16):
    result = spread * jax.random.normal(stream_key, shape, jnp.float32)
    if split:
        result = result * steps_of(stream_key, shape, split, -0.22, 0.18)
    return jnp.clip(result, -bound, bound).astype(kind)


def gaussian_with(own_key, extent, scale, limit, cuts, heavy, kind=jnp.bfloat16):
    values = scale * jax.random.normal(own_key, extent, jnp.float32)
    if cuts:
        values = values * steps_of(own_key, extent, cuts, -0.22, 0.18)
    return jnp.clip(with_spikes(values, jax.random.fold_in(own_key, 3), *heavy), -limit, limit).astype(kind)


def setup_inputs(seed: int = 0) -> dict:
    arg_keys = jax.random.split(jax.random.key(seed), 9)
    inputs = gaussian_with(arg_keys[0], (N_GROUP, N_SHUF * ROWS, D), 1.0, 8.0, ((0, 8), (1, 4)), (0, 2, 8, 2.0))
    cotangent = noise(arg_keys[1], (N_GROUP, N_SHUF * ROWS, D), 1.0, 8.0, ((0, 8), (1, 4)))
    w_uvqk = noise(arg_keys[2], (D, 4 * D), D ** -0.5, 0.25, ((0, 8),))
    w_out = noise(arg_keys[3], (D, D), D ** -0.5, 0.25, ((0, 8),))
    send_perm = jax.vmap(lambda own: jax.random.permutation(own, BLK_DEV))(jax.random.split(arg_keys[4], N_GROUP * N_SHUF)).reshape((N_GROUP, N_SHUF, BLK_DEV)).astype(jnp.int32)
    recv_perm = jax.vmap(lambda own: jax.random.permutation(own, BLK_DEV))(jax.random.split(arg_keys[5], N_GROUP * N_SHUF)).reshape((N_GROUP, N_SHUF, BLK_DEV)).astype(jnp.int32)
    lengths = jax.vmap(lambda own: ragged_sizes(own, USERS, ROWS, MAX_LEN, 2))(jax.random.split(arg_keys[6], N_GROUP * N_SHUF)).reshape((N_GROUP, N_SHUF, USERS)).astype(jnp.int32)
    prefixes = set_ends(jax.random.randint(arg_keys[7], (N_GROUP, N_SHUF, USERS), 0, MAX_LEN // 4 + 1), jax.random.fold_in(arg_keys[7], 1), 0, (MAX_LEN // 4 + 1) - 1).astype(jnp.int32)
    return dict(inputs=inputs, cotangent=cotangent, w_uvqk=w_uvqk, w_out=w_out, send_perm=send_perm, recv_perm=recv_perm, lengths=lengths, prefixes=prefixes)


norm_eps = 1e-05

def normalize(values):
    center = lax.optimization_barrier(jnp.mean(values, axis=-1, keepdims=True))
    centred = values - center
    variance = lax.optimization_barrier(jnp.mean(centred * centred, axis=-1, keepdims=True))
    inv_scale = lax.rsqrt(variance + norm_eps)
    return (centred * inv_scale, inv_scale)

def silu_slope(values):
    sigma = jax.nn.sigmoid(values)
    return sigma * (1.0 + values * (1.0 - sigma))

def visible(user_lengths, user_prefixes, row_count):
    user_ends = jnp.cumsum(user_lengths).astype(jnp.int32)
    row_index = jnp.arange(row_count, dtype=jnp.int32)
    user_index = lax.optimization_barrier(jnp.sum((row_index[:, None] >= user_ends[None, :]).astype(jnp.int32), axis=1)).astype(jnp.int32)
    member = user_index[:, None] == jnp.arange(user_lengths.shape[0], dtype=jnp.int32)[None, :]
    starts = (user_ends - user_lengths).astype(jnp.int32)
    position = row_index - lax.optimization_barrier(jnp.sum(jnp.where(member, starts[None, :], 0), axis=1)).astype(jnp.int32)
    prefix_len = lax.optimization_barrier(jnp.sum(jnp.where(member, user_prefixes[None, :], 0), axis=1)).astype(jnp.int32)
    same_user = user_index[:, None] == user_index[None, :]
    return same_user & ((row_index[None, :] <= row_index[:, None]) | (position[None, :] < prefix_len[:, None]))

def attention(activated, weight_out, residual, allowed):
    row_count = activated.shape[0]
    gate_u = activated[:, :D]
    values = activated[:, D:2 * D].reshape(row_count, HEADS, D // HEADS)
    queries = activated[:, 2 * D:3 * D].reshape(row_count, HEADS, D // HEADS)
    keys = activated[:, 3 * D:].reshape(row_count, HEADS, D // HEADS)
    scores = jnp.einsum('qhd,khd->hqk', queries.astype(jnp.float32), keys.astype(jnp.float32))
    weights = (jnp.where(allowed[None], jax.nn.silu(scores), 0.0) / ROWS).astype(jnp.bfloat16)
    mixed = jnp.einsum('hqk,khd->qhd', weights.astype(jnp.float32), values.astype(jnp.float32)).reshape(row_count, D)
    normed, unused = normalize(mixed)
    gated = (normed * gate_u.astype(jnp.float32)).astype(jnp.bfloat16)
    return (jnp.dot(gated, weight_out, preferred_element_type=jnp.float32) + residual).astype(jnp.bfloat16)

def device_pass(rows_x, rows_cot, w_uvqk, w_out, user_lengths, user_prefixes):
    inputs_f32 = rows_x.astype(jnp.float32)
    centred, inv_scale = normalize(inputs_f32)
    normed_x = centred.astype(jnp.bfloat16)
    projected = jnp.dot(normed_x, w_uvqk, preferred_element_type=jnp.float32)
    activated = jax.nn.silu(projected).astype(jnp.bfloat16)
    allowed = visible(user_lengths, user_prefixes, rows_x.shape[0])
    layer_value, pullback = jax.vjp(partial(attention, allowed=allowed), activated, w_out, inputs_f32)
    grad_act, grad_weight, grad_res = pullback(rows_cot)
    grad_proj = (grad_act.astype(jnp.float32) * silu_slope(projected)).astype(jnp.bfloat16)
    part_uvqk = lax.dot_general(normed_x, grad_proj, (((0,), (0,)), ((), ())), preferred_element_type=jnp.float32)
    grad_normed = lax.dot_general(grad_proj, w_uvqk, (((1,), (1,)), ((), ())), preferred_element_type=jnp.float32)
    grad_center = lax.optimization_barrier(jnp.mean(grad_normed, axis=-1, keepdims=True))
    grad_proj_z = lax.optimization_barrier(jnp.mean(grad_normed * centred, axis=-1, keepdims=True))
    grad_rows = inv_scale * (grad_normed - grad_center - centred * grad_proj_z) + grad_res.astype(jnp.float32)
    return (layer_value, grad_rows.astype(jnp.bfloat16), part_uvqk, grad_weight.astype(jnp.float32))

def reference(inputs, cotangent, w_uvqk, w_out, send_perm, recv_perm, lengths, prefixes):
    groups = N_GROUP
    peers = N_SHUF
    blocks = BLK_DEV
    input_blocks = inputs.reshape(groups, peers * blocks, BLOCK, D)
    cot_blocks = cotangent.reshape(groups, peers * blocks, BLOCK, D)
    source_dev = (recv_perm // CAP).astype(jnp.int32)
    sub_slot = (recv_perm % CAP).astype(jnp.int32)
    target = jnp.arange(peers, dtype=jnp.int32)[None, :, None]
    send_pos = (target * CAP + sub_slot).astype(jnp.int32)
    group_index = jnp.arange(groups, dtype=jnp.int32)[:, None, None]
    block_id = send_perm[group_index, source_dev, send_pos]
    src_flat = (source_dev * blocks + block_id).reshape(groups, peers * blocks).astype(jnp.int32)
    bal_x = jnp.take_along_axis(input_blocks, src_flat[:, :, None, None], axis=1).reshape(groups * peers, ROWS, D)
    bal_cot = jnp.take_along_axis(cot_blocks, src_flat[:, :, None, None], axis=1).reshape(groups * peers, ROWS, D)
    user_lens = lengths.reshape(groups * peers, USERS)
    user_pref = prefixes.reshape(groups * peers, USERS)

    def step(totals, device_items):
        layer_value, grad_rows, part_uvqk, part_wout = device_pass(device_items[0], device_items[1], w_uvqk, w_out, device_items[2], device_items[3])
        rounded = lax.optimization_barrier(part_uvqk.astype(jnp.bfloat16)).astype(jnp.float32)
        return ((totals[0] + rounded, totals[1] + part_wout), (layer_value, grad_rows))
    start_totals = (jnp.zeros((D, 4 * D), jnp.float32), jnp.zeros((D, D), jnp.float32))
    totals, outputs = lax.scan(step, start_totals, (bal_x, bal_cot, user_lens, user_pref))
    inverse_map = jnp.zeros((groups, peers * blocks), jnp.int32).at[jnp.arange(groups, dtype=jnp.int32)[:, None], src_flat].set(jnp.broadcast_to(jnp.arange(peers * blocks, dtype=jnp.int32)[None, :], (groups, peers * blocks)))
    out_blocks = outputs[0].reshape(groups, peers * blocks, BLOCK, D)
    grad_blocks = outputs[1].reshape(groups, peers * blocks, BLOCK, D)
    layer_out = jnp.take_along_axis(out_blocks, inverse_map[:, :, None, None], axis=1).reshape(groups, peers * ROWS, D)
    grad_input = jnp.take_along_axis(grad_blocks, inverse_map[:, :, None, None], axis=1).reshape(groups, peers * ROWS, D)
    return (layer_out, grad_input, totals[0], totals[1])
```

```python
from functools import partial

import jax
import jax.numpy as jnp
from jax import lax
from jax.experimental import pallas as pl
from jax.experimental.pallas import tpu as pltpu
from jax.sharding import PartitionSpec as P

HEADS = 8
norm_eps = 1e-05
F32 = jnp.float32
BF16 = jnp.bfloat16
VMEM = pl.BlockSpec(memory_space=pltpu.VMEM)
SMEM = pl.BlockSpec(memory_space=pltpu.SMEM)
NN = (((1,), (0,)), ((), ()))
NT = (((1,), (1,)), ((), ()))
TN = (((0,), (0,)), ((), ()))


def dot(a, b, dims=NN):
    return lax.dot_general(a, b, dims, preferred_element_type=F32)


def sigmoid(values):
    return 0.5 * jnp.tanh(0.5 * values) + 0.5


def normalize(values):
    center = jnp.mean(values, axis=-1, keepdims=True)
    centred = values - center
    variance = jnp.mean(centred * centred, axis=-1, keepdims=True)
    inv_scale = lax.rsqrt(variance + norm_eps)
    return (centred * inv_scale, inv_scale)


def exchange(value, axis, size, mask):
    return lax.ppermute(value, axis, [(i, i ^ mask) for i in range(size)])


def global_row(index, me, chunk):
    place = lax.div(index, chunk)
    return (me ^ place) * chunk + (index - place * chunk)


def looked_up(order_ref, row):
    blocks = order_ref.shape[1]
    block = row.shape[0] // blocks
    at = lax.div(row, block)
    lane = lax.broadcasted_iota(jnp.int32, (row.shape[0], blocks), 1)
    picked = jnp.where(at == lane, order_ref[...], 0).astype(F32)
    found = jnp.sum(picked, axis=1, keepdims=True).astype(jnp.int32)
    return found * block + (row - at * block)


def send_matrix(order_ref, me, rows, chunk):
    row = lax.broadcasted_iota(jnp.int32, (rows, 1), 0)
    source = looked_up(order_ref, global_row(row, me, chunk))
    lane = lax.broadcasted_iota(jnp.int32, (rows, rows), 1)
    return (source == lane).astype(F32).astype(BF16)


def recv_matrix(order_ref, me, rows, chunk):
    row = lax.broadcasted_iota(jnp.int32, (rows, 1), 0)
    source = looked_up(order_ref, row)
    lane = lax.broadcasted_iota(jnp.int32, (rows, rows), 1)
    return (source == global_row(lane, me, chunk)).astype(F32).astype(BF16)


def stacked(refs, which):
    return jnp.concatenate([ref[which] for ref in refs], axis=0)


def pre_kernel(parts, me_ref, order_ref, x_ref, cot_ref, uvqk_ref, out_ref, w_ref, *send_refs):
    rows = x_ref.shape[0]
    columns = uvqk_ref.shape[1]
    w_ref[:, :columns] = uvqk_ref[...]
    w_ref[:, columns:] = out_ref[...]
    matrix = send_matrix(order_ref, me_ref[0], rows, rows // parts)
    step = rows // len(send_refs)
    for which, ref in enumerate((x_ref, cot_ref)):
        ordered = dot(matrix, ref[...]).astype(BF16)
        for k, send in enumerate(send_refs):
            send[which] = ordered[k * step : (k + 1) * step]


def post_kernel(parts, me_ref, order_ref, *refs):
    back_refs, (out_ref, grad_ref) = refs[:-2], refs[-2:]
    rows = out_ref.shape[0]
    matrix = send_matrix(order_ref, me_ref[0], rows, rows // parts)
    for which, ref in enumerate((out_ref, grad_ref)):
        ref[...] = dot(matrix, stacked(back_refs, which), TN).astype(BF16)


def layer_kernel(
    parts,
    groups,
    n_rows,
    me_ref,
    lengths_ref,
    prefixes_ref,
    order_ref,
    *refs,
):
    row_refs, refs = refs[:n_rows], refs[n_rows:]
    weight_refs, refs = refs[:groups], refs[groups:]
    back_refs, refs = refs[:n_rows], refs[n_rows:]
    keep_ref, give_ref, refs = refs[0], refs[1], refs[2:]
    w_ref, xt_ref, gt_ref, act_ref, slope_ref, mix_ref, weights_ref, bend_ref, gproj_ref = refs
    rows, width = mix_ref.shape
    shard = width // groups
    group_me, shuf_me = me_ref[1], me_ref[0]

    matrix = recv_matrix(order_ref, shuf_me, rows, rows // parts)
    x = dot(matrix, stacked(row_refs, 0))
    cot = dot(matrix, stacked(row_refs, 1))
    cot_b = cot.astype(BF16)
    z, inv_scale = normalize(x)
    xn = z.astype(BF16)
    xt_ref[...] = xn.T

    def shard_rows(k):
        return pl.ds(pl.multiple_of((group_me ^ k) * shard, shard), shard)

    for k in range(groups):
        w_ref[shard_rows(k), :] = weight_refs[k][...]

    for c in range(4):
        cols = slice(c * width, (c + 1) * width)
        projected = dot(xn, w_ref[:, cols])
        s = sigmoid(projected)
        act = projected * s
        act_ref[:, cols] = act.astype(BF16)
        slope_ref[:, cols] = s + act * (1.0 - s)

    row = lax.broadcasted_iota(jnp.int32, (rows, 1), 0)
    low = jnp.zeros((rows, 1), jnp.int32)
    high = jnp.zeros((rows, 1), jnp.int32)
    start = jnp.int32(0)
    for u in range(lengths_ref.shape[0]):
        end = start + lengths_ref[u]
        mine = (row >= start) & (row < end)
        reach = jnp.minimum(end, jnp.maximum(row + 1, start + prefixes_ref[u]))
        low = jnp.where(mine, start, low)
        high = jnp.where(mine, reach, high)
        start = end
    lane = lax.broadcasted_iota(jnp.int32, (rows, rows), 1)
    scale = jnp.where((lane >= low) & (lane < high), 1.0 / rows, 0.0)

    head_width = width // HEADS
    per = max(1, 128 // head_width)
    wide = per * head_width
    place = lax.div(lax.broadcasted_iota(jnp.int32, (rows, wide), 1), head_width)

    def only(value, h):
        return jnp.where(place == h, value, jnp.zeros_like(value)) if per > 1 else value

    def cut(ref, block, g):
        return ref[:, block * width + g * wide : block * width + (g + 1) * wide]

    for g in range(HEADS // per):
        v, q, k = cut(act_ref, 1, g), cut(act_ref, 2, g), cut(act_ref, 3, g)
        mixed = jnp.zeros((rows, wide), F32)
        for h in range(per):
            scores = dot(only(q, h), k, NT)
            s = sigmoid(scores)
            value = scores * s
            weights = (value * scale).astype(BF16)
            weights_ref[g * per + h] = weights
            bend_ref[g * per + h] = (s + value * (1.0 - s)) * scale
            mixed += dot(weights, only(v, h))
        mix_ref[:, g * wide : (g + 1) * wide] = mixed

    normed, mix_inv = normalize(mix_ref[...])
    gate = act_ref[:, :width].astype(F32)
    gated = (normed * gate).astype(BF16)
    gt_ref[...] = gated.T
    w_out = w_ref[:, 4 * width :]
    out = (dot(gated, w_out) + x).astype(BF16)

    g_gated = dot(cot_b, w_out, NT).astype(BF16).astype(F32)
    gproj_ref[:, :width] = ((g_gated * normed).astype(BF16).astype(F32) * slope_ref[:, :width]).astype(BF16)
    g_normed = g_gated * gate
    g_mixed = mix_inv * (
        g_normed
        - jnp.mean(g_normed, axis=-1, keepdims=True)
        - normed * jnp.mean(g_normed * normed, axis=-1, keepdims=True)
    )
    mix_ref[...] = g_mixed

    for g in range(HEADS // per):
        v, q, k = cut(act_ref, 1, g), cut(act_ref, 2, g), cut(act_ref, 3, g)
        g_mix = mix_ref[:, g * wide : (g + 1) * wide].astype(BF16)
        g_v = jnp.zeros((rows, wide), F32)
        g_q = jnp.zeros((rows, wide), F32)
        g_k = jnp.zeros((rows, wide), F32)
        for h in range(per):
            mine = only(g_mix, h)
            g_weights = dot(mine, v, NT).astype(BF16).astype(F32)
            g_scores = (g_weights * bend_ref[g * per + h]).astype(BF16)
            g_v += dot(weights_ref[g * per + h], mine, TN)
            g_q += dot(g_scores, only(k, h))
            g_k += dot(g_scores, only(q, h), TN)
        for block, value in ((1, g_v), (2, g_q), (3, g_k)):
            at = slice(block * width + g * wide, block * width + (g + 1) * wide)
            gproj_ref[:, at] = (value.astype(BF16).astype(F32) * slope_ref[:, at]).astype(BF16)

    for which, ref in ((0, keep_ref), (1, give_ref)):
        picked = [2 * m + which for m in range(groups // 2)]
        lhs = jnp.concatenate([xt_ref[shard_rows(k), :] for k in picked], axis=0)
        lhs_out = jnp.concatenate([gt_ref[shard_rows(k), :] for k in picked], axis=0)
        for c in range(4):
            cols = slice(c * width, (c + 1) * width)
            ref[:, cols] = dot(lhs, gproj_ref[:, cols]).astype(BF16)
        ref[:, 4 * width :] = dot(lhs_out, cot_b).astype(BF16)

    g_xn = dot(gproj_ref[...], w_ref[:, : 4 * width], NT)
    g_x = (
        inv_scale
        * (
            g_xn
            - jnp.mean(g_xn, axis=-1, keepdims=True)
            - z * jnp.mean(g_xn * z, axis=-1, keepdims=True)
        )
        + cot
    ).astype(BF16)
    step = rows // n_rows
    for which, value in ((0, out), (1, g_x)):
        back = dot(matrix, value, TN).astype(BF16)
        for k, ref in enumerate(back_refs):
            ref[which] = back[k * step : (k + 1) * step]


def on_device(groups, parts, inputs, cotangent, w_uvqk, w_out, send_perm, recv_perm, lengths, prefixes):
    rows, width = inputs.shape[1:]
    shard = w_uvqk.shape[0]
    columns = w_uvqk.shape[1] + w_out.shape[1]
    chunk = rows // parts
    whole_tiles = chunk % 16 == 0
    n_rows = parts if whole_tiles else 1
    me = jnp.stack([lax.axis_index("shuf"), lax.axis_index("group")]).astype(jnp.int32)
    send_order, recv_order = send_perm[0], recv_perm[0]
    limit = pltpu.CompilerParams(vmem_limit_bytes=40 * 1024 * 1024)
    rows_shape = jax.ShapeDtypeStruct((2, rows // n_rows, width), BF16)

    def swap_rows(pieces):
        if not whole_tiles:
            cut = pieces[0].reshape(2, parts, chunk, width)
            pieces = [cut[:, k] for k in range(parts)]
        moved = [pieces[0]] + [exchange(pieces[k], "shuf", parts, k) for k in range(1, parts)]
        return moved if whole_tiles else [jnp.concatenate(moved, axis=1)]

    w_mine, *outgoing = pl.pallas_call(
        partial(pre_kernel, parts),
        out_shape=[jax.ShapeDtypeStruct((shard, columns), BF16)] + [rows_shape] * n_rows,
        in_specs=[SMEM] + [VMEM] * 5,
        out_specs=[VMEM] * (1 + n_rows),
        compiler_params=limit,
        name="pre",
    )(me, send_order, inputs[0], cotangent[0], w_uvqk, w_out)

    shards = [None] * groups
    for k in range(0, groups, 2):
        shards[k] = w_mine if k == 0 else exchange(w_mine, "group", groups, k)
    for k in range(0, groups, 2):
        shards[k + 1] = exchange(shards[k], "group", groups, 1)
    arrived = swap_rows(outgoing)

    half = groups // 2 * shard
    *returning, keep, give = pl.pallas_call(
        partial(layer_kernel, parts, groups, n_rows),
        out_shape=[rows_shape] * n_rows + [jax.ShapeDtypeStruct((half, columns), BF16)] * 2,
        in_specs=[SMEM] * 3 + [VMEM] * (1 + n_rows + groups),
        out_specs=[VMEM] * (n_rows + 2),
        scratch_shapes=[
            pltpu.VMEM((width, columns), BF16),
            pltpu.VMEM((width, rows), BF16),
            pltpu.VMEM((width, rows), BF16),
            pltpu.VMEM((rows, 4 * width), BF16),
            pltpu.VMEM((rows, 4 * width), F32),
            pltpu.VMEM((rows, width), F32),
            pltpu.VMEM((HEADS, rows, rows), BF16),
            pltpu.VMEM((HEADS, rows, rows), F32),
            pltpu.VMEM((rows, 4 * width), BF16),
        ],
        compiler_params=limit,
        name="layer",
    )(me, lengths[0, 0], prefixes[0, 0], recv_order, *arrived, *shards)

    taken = exchange(give, "group", groups, 1)
    chip = (keep.astype(F32) + taken.astype(F32)).astype(BF16).reshape(groups // 2, shard, columns)
    total = chip[0].astype(F32)
    for m in range(1, groups // 2):
        total = total + exchange(chip[m], "group", groups, 2 * m).astype(F32)
    masks = [2 ** (j + 1) - 1 for j in range(parts.bit_length() - 1)]
    first, second = total[: shard // 2].astype(BF16), total[shard // 2 :].astype(BF16)
    for mask_a, mask_b in zip(masks, reversed(masks)):
        first_f32 = first.astype(F32) + exchange(first, "shuf", parts, mask_a).astype(F32)
        second_f32 = second.astype(F32) + exchange(second, "shuf", parts, mask_b).astype(F32)
        first, second = first_f32.astype(BF16), second_f32.astype(BF16)
    total = jnp.concatenate([first_f32, second_f32], axis=0)
    grad_uvqk, grad_wout = total[:, : w_uvqk.shape[1]], total[:, w_uvqk.shape[1] :]

    owner_out, owner_grad = pl.pallas_call(
        partial(post_kernel, parts),
        out_shape=[jax.ShapeDtypeStruct((rows, width), BF16)] * 2,
        in_specs=[SMEM] + [VMEM] * (1 + n_rows),
        out_specs=[VMEM] * 2,
        compiler_params=limit,
        name="post",
    )(me, send_order, *swap_rows(returning))
    return (owner_out[None], owner_grad[None], grad_uvqk, grad_wout)


def solution(mesh):
    data, weight = P("group", "shuf", None), P("group", None)
    return jax.shard_map(
        partial(on_device, mesh.shape["group"], mesh.shape["shuf"]),
        mesh=mesh,
        in_specs=(data, data, weight, weight, data, data, data, data),
        out_specs=(data, data, weight, weight),
        check_vma=False,
    )
```

```python
from functools import partial

import jax
import jax.numpy as jnp
from jax import lax
from jax.experimental import pallas as pl
from jax.experimental.pallas import tpu as pltpu
from jax.sharding import PartitionSpec as P

HEADS = 8
norm_eps = 1e-05
F32 = jnp.float32
BF16 = jnp.bfloat16
VMEM = pl.BlockSpec(memory_space=pltpu.VMEM)
SMEM = pl.BlockSpec(memory_space=pltpu.SMEM)
HBM = pl.BlockSpec(memory_space=pltpu.HBM)
NN = (((1,), (0,)), ((), ()))
NT = (((1,), (1,)), ((), ()))
TN = (((0,), (0,)), ((), ()))


def dot(a, b, dims=NN):
    return lax.dot_general(a, b, dims, preferred_element_type=F32)


def sigmoid(values):
    return 0.5 * jnp.tanh(0.5 * values) + 0.5


def normalize(values):
    center = jnp.mean(values, axis=-1, keepdims=True)
    centred = values - center
    variance = jnp.mean(centred * centred, axis=-1, keepdims=True)
    inv_scale = lax.rsqrt(variance + norm_eps)
    return (centred * inv_scale, inv_scale)


def exchange(value, axis, size, mask):
    return lax.ppermute(value, axis, [(i, i ^ mask) for i in range(size)])


def global_row(index, me, chunk):
    place = lax.div(index, chunk)
    return (me ^ place) * chunk + (index - place * chunk)


def looked_up(order_ref, row):
    blocks = order_ref.shape[1]
    block = row.shape[0] // blocks
    at = lax.div(row, block)
    lane = lax.broadcasted_iota(jnp.int32, (row.shape[0], blocks), 1)
    picked = jnp.where(at == lane, order_ref[...], 0).astype(F32)
    found = jnp.sum(picked, axis=1, keepdims=True).astype(jnp.int32)
    return found * block + (row - at * block)


def send_matrix(order_ref, me, rows, chunk):
    row = lax.broadcasted_iota(jnp.int32, (rows, 1), 0)
    source = looked_up(order_ref, global_row(row, me, chunk))
    lane = lax.broadcasted_iota(jnp.int32, (rows, rows), 1)
    return (source == lane).astype(F32).astype(BF16)


def recv_matrix(order_ref, me, rows, chunk):
    row = lax.broadcasted_iota(jnp.int32, (rows, 1), 0)
    source = looked_up(order_ref, row)
    lane = lax.broadcasted_iota(jnp.int32, (rows, rows), 1)
    return (source == global_row(lane, me, chunk)).astype(F32).astype(BF16)


def stacked(refs, which):
    return jnp.concatenate([ref[which] for ref in refs], axis=0)


def pre_kernel(parts, me_ref, order_in, x_in, cot_in, uvqk_in, out_in, w_ref, *refs):
    send_refs, (order_ref, x_ref, cot_ref, sem) = refs[:-4], refs[-4:]
    rows = x_ref.shape[0]
    columns = uvqk_in.shape[1]
    moves = (
        (order_in, order_ref),
        (x_in, x_ref),
        (cot_in, cot_ref),
        (uvqk_in, w_ref.at[:, :columns]),
        (out_in, w_ref.at[:, columns:]),
    )
    copies = [pltpu.make_async_copy(a, b, sem.at[n]) for n, (a, b) in enumerate(moves)]
    for copy in copies:
        copy.start()
    for copy in copies:
        copy.wait()
    matrix = send_matrix(order_ref, me_ref[0], rows, rows // parts)
    step = rows // len(send_refs)
    for which, ref in enumerate((x_ref, cot_ref)):
        ordered = dot(matrix, ref[...]).astype(BF16)
        for k, send in enumerate(send_refs):
            send[which] = ordered[k * step : (k + 1) * step]


def plan_kernel(parts, me_ref, order_in, lengths_in, prefixes_in, matrix_ref, scale_ref, *refs):
    order_ref, lengths_ref, prefixes_ref, sem = refs
    rows = matrix_ref.shape[0]
    moves = ((order_in, order_ref), (lengths_in, lengths_ref), (prefixes_in, prefixes_ref))
    copies = [pltpu.make_async_copy(a, b, sem.at[n]) for n, (a, b) in enumerate(moves)]
    for copy in copies:
        copy.start()
    for copy in copies:
        copy.wait()
    matrix_ref[...] = recv_matrix(order_ref, me_ref[0], rows, rows // parts)
    row = lax.broadcasted_iota(jnp.int32, (rows, 1), 0)
    low = jnp.zeros((rows, 1), jnp.int32)
    high = jnp.zeros((rows, 1), jnp.int32)
    start = jnp.int32(0)
    for u in range(lengths_ref.shape[1]):
        end = start + lengths_ref[0, u]
        mine = (row >= start) & (row < end)
        reach = jnp.minimum(end, jnp.maximum(row + 1, start + prefixes_ref[0, u]))
        low = jnp.where(mine, start, low)
        high = jnp.where(mine, reach, high)
        start = end
    lane = lax.broadcasted_iota(jnp.int32, (rows, rows), 1)
    scale_ref[...] = jnp.where((lane >= low) & (lane < high), 1.0 / rows, 0.0)


def post_kernel(parts, me_ref, order_ref, *refs):
    back_refs, (out_ref, grad_ref) = refs[:-2], refs[-2:]
    rows = out_ref.shape[0]
    matrix = send_matrix(order_ref, me_ref[0], rows, rows // parts)
    for which, ref in enumerate((out_ref, grad_ref)):
        ref[...] = dot(matrix, stacked(back_refs, which), TN).astype(BF16)


def layer_kernel(
    parts,
    groups,
    n_rows,
    me_ref,
    matrix_ref,
    scale_ref,
    *refs,
):
    row_refs, refs = refs[:n_rows], refs[n_rows:]
    weight_refs, refs = refs[:groups], refs[groups:]
    back_refs, refs = refs[:n_rows], refs[n_rows:]
    keep_ref, give_ref, refs = refs[0], refs[1], refs[2:]
    w_ref, xt_ref, gt_ref, act_ref, slope_ref, mix_ref, weights_ref, bend_ref, gproj_ref = refs
    rows, width = mix_ref.shape
    shard = width // groups
    group_me = me_ref[1]

    matrix = matrix_ref[...]
    x = dot(matrix, stacked(row_refs, 0))
    cot = dot(matrix, stacked(row_refs, 1))
    cot_b = cot.astype(BF16)
    z, inv_scale = normalize(x)
    xn = z.astype(BF16)
    xt_ref[...] = xn.T

    def shard_rows(k):
        return pl.ds(pl.multiple_of((group_me ^ k) * shard, shard), shard)

    for k in range(groups):
        w_ref[shard_rows(k), :] = weight_refs[k][...]

    for c in range(4):
        cols = slice(c * width, (c + 1) * width)
        projected = dot(xn, w_ref[:, cols])
        s = sigmoid(projected)
        act = projected * s
        act_ref[:, cols] = act.astype(BF16)
        slope_ref[:, cols] = s + act * (1.0 - s)

    scale = scale_ref[...]
    head_width = width // HEADS
    per = max(1, 128 // head_width)
    wide = per * head_width
    place = lax.div(lax.broadcasted_iota(jnp.int32, (rows, wide), 1), head_width)

    def only(value, h):
        return jnp.where(place == h, value, jnp.zeros_like(value)) if per > 1 else value

    def cut(ref, block, g):
        return ref[:, block * width + g * wide : block * width + (g + 1) * wide]

    for g in range(HEADS // per):
        v, q, k = cut(act_ref, 1, g), cut(act_ref, 2, g), cut(act_ref, 3, g)
        mixed = jnp.zeros((rows, wide), F32)
        for h in range(per):
            scores = dot(only(q, h), k, NT)
            s = sigmoid(scores)
            value = scores * s
            weights = (value * scale).astype(BF16)
            weights_ref[g * per + h] = weights
            bend_ref[g * per + h] = (s + value * (1.0 - s)) * scale
            mixed += dot(weights, only(v, h))
        mix_ref[:, g * wide : (g + 1) * wide] = mixed

    normed, mix_inv = normalize(mix_ref[...])
    gate = act_ref[:, :width].astype(F32)
    gated = (normed * gate).astype(BF16)
    gt_ref[...] = gated.T
    w_out = w_ref[:, 4 * width :]
    out = (dot(gated, w_out) + x).astype(BF16)

    g_gated = dot(cot_b, w_out, NT).astype(BF16).astype(F32)
    gproj_ref[:, :width] = ((g_gated * normed).astype(BF16).astype(F32) * slope_ref[:, :width]).astype(BF16)
    g_normed = g_gated * gate
    g_mixed = mix_inv * (
        g_normed
        - jnp.mean(g_normed, axis=-1, keepdims=True)
        - normed * jnp.mean(g_normed * normed, axis=-1, keepdims=True)
    )
    mix_ref[...] = g_mixed

    for g in range(HEADS // per):
        v, q, k = cut(act_ref, 1, g), cut(act_ref, 2, g), cut(act_ref, 3, g)
        g_mix = mix_ref[:, g * wide : (g + 1) * wide].astype(BF16)
        g_v = jnp.zeros((rows, wide), F32)
        g_q = jnp.zeros((rows, wide), F32)
        g_k = jnp.zeros((rows, wide), F32)
        for h in range(per):
            mine = only(g_mix, h)
            g_weights = dot(mine, v, NT).astype(BF16).astype(F32)
            g_scores = (g_weights * bend_ref[g * per + h]).astype(BF16)
            g_v += dot(weights_ref[g * per + h], mine, TN)
            g_q += dot(g_scores, only(k, h))
            g_k += dot(g_scores, only(q, h), TN)
        for block, value in ((1, g_v), (2, g_q), (3, g_k)):
            at = slice(block * width + g * wide, block * width + (g + 1) * wide)
            gproj_ref[:, at] = (value.astype(BF16).astype(F32) * slope_ref[:, at]).astype(BF16)

    for which, ref in ((0, keep_ref), (1, give_ref)):
        picked = [2 * m + which for m in range(groups // 2)]
        lhs = jnp.concatenate([xt_ref[shard_rows(k), :] for k in picked], axis=0)
        lhs_out = jnp.concatenate([gt_ref[shard_rows(k), :] for k in picked], axis=0)
        for c in range(4):
            cols = slice(c * width, (c + 1) * width)
            ref[:, cols] = dot(lhs, gproj_ref[:, cols]).astype(BF16)
        ref[:, 4 * width :] = dot(lhs_out, cot_b).astype(BF16)

    g_xn = dot(gproj_ref[...], w_ref[:, : 4 * width], NT)
    g_x = (
        inv_scale
        * (
            g_xn
            - jnp.mean(g_xn, axis=-1, keepdims=True)
            - z * jnp.mean(g_xn * z, axis=-1, keepdims=True)
        )
        + cot
    ).astype(BF16)
    step = rows // n_rows
    for which, value in ((0, out), (1, g_x)):
        back = dot(matrix, value, TN).astype(BF16)
        for k, ref in enumerate(back_refs):
            ref[which] = back[k * step : (k + 1) * step]


def on_device(groups, parts, inputs, cotangent, w_uvqk, w_out, send_perm, recv_perm, lengths, prefixes):
    rows, width = inputs.shape[1:]
    shard = w_uvqk.shape[0]
    columns = w_uvqk.shape[1] + w_out.shape[1]
    chunk = rows // parts
    whole_tiles = chunk % 16 == 0
    n_rows = parts if whole_tiles else 1
    me = jnp.stack([lax.axis_index("shuf"), lax.axis_index("group")]).astype(jnp.int32)
    send_order, recv_order = send_perm[0], recv_perm[0]
    limit = pltpu.CompilerParams(vmem_limit_bytes=40 * 1024 * 1024)
    rows_shape = jax.ShapeDtypeStruct((2, rows // n_rows, width), BF16)

    def swap_rows(pieces):
        if not whole_tiles:
            cut = pieces[0].reshape(2, parts, chunk, width)
            pieces = [cut[:, k] for k in range(parts)]
        moved = [pieces[0]] + [exchange(pieces[k], "shuf", parts, k) for k in range(1, parts)]
        return moved if whole_tiles else [jnp.concatenate(moved, axis=1)]

    w_mine, *outgoing = pl.pallas_call(
        partial(pre_kernel, parts),
        out_shape=[jax.ShapeDtypeStruct((shard, columns), BF16)] + [rows_shape] * n_rows,
        in_specs=[SMEM] + [HBM] * 5,
        out_specs=[VMEM] * (1 + n_rows),
        scratch_shapes=[
            pltpu.VMEM(send_order.shape, jnp.int32),
            pltpu.VMEM((rows, width), BF16),
            pltpu.VMEM((rows, width), BF16),
            pltpu.SemaphoreType.DMA((5,)),
        ],
        compiler_params=limit,
        name="pre",
    )(me, send_order, inputs[0], cotangent[0], w_uvqk, w_out)

    matrix, scale = pl.pallas_call(
        partial(plan_kernel, parts),
        out_shape=[jax.ShapeDtypeStruct((rows, rows), BF16), jax.ShapeDtypeStruct((rows, rows), F32)],
        in_specs=[SMEM] + [HBM] * 3,
        out_specs=[VMEM] * 2,
        scratch_shapes=[
            pltpu.VMEM(recv_order.shape, jnp.int32),
            pltpu.SMEM(lengths[0].shape, jnp.int32),
            pltpu.SMEM(prefixes[0].shape, jnp.int32),
            pltpu.SemaphoreType.DMA((3,)),
        ],
        compiler_params=limit,
        name="plan",
    )(me, recv_order, lengths[0], prefixes[0])

    near = [w_mine] + [exchange(w_mine, "group", groups, k) for k in range(2, groups, 2)]
    near, arrived, matrix, scale = lax.optimization_barrier((near, swap_rows(outgoing), matrix, scale))
    shards = [s for mine in near for s in (mine, exchange(mine, "group", groups, 1))]

    half = groups // 2 * shard
    *returning, keep, give = pl.pallas_call(
        partial(layer_kernel, parts, groups, n_rows),
        out_shape=[rows_shape] * n_rows + [jax.ShapeDtypeStruct((half, columns), BF16)] * 2,
        in_specs=[SMEM] + [VMEM] * (2 + n_rows + groups),
        out_specs=[VMEM] * (n_rows + 2),
        scratch_shapes=[
            pltpu.VMEM((width, columns), BF16),
            pltpu.VMEM((width, rows), BF16),
            pltpu.VMEM((width, rows), BF16),
            pltpu.VMEM((rows, 4 * width), BF16),
            pltpu.VMEM((rows, 4 * width), F32),
            pltpu.VMEM((rows, width), F32),
            pltpu.VMEM((HEADS, rows, rows), BF16),
            pltpu.VMEM((HEADS, rows, rows), F32),
            pltpu.VMEM((rows, 4 * width), BF16),
        ],
        compiler_params=limit,
        name="layer",
    )(me, matrix, scale, *arrived, *shards)

    taken = exchange(give, "group", groups, 1)
    chip = (keep.astype(F32) + taken.astype(F32)).astype(BF16).reshape(groups // 2, shard, columns)
    others = [exchange(chip[m], "group", groups, 2 * m) for m in range(1, groups // 2)]
    others, returned = lax.optimization_barrier((others, swap_rows(returning)))
    total = chip[0].astype(F32) + sum(other.astype(F32) for other in others)
    masks = [2 ** (j + 1) - 1 for j in range(parts.bit_length() - 1)]
    first, second = total[: shard // 2].astype(BF16), total[shard // 2 :].astype(BF16)
    for mask_a, mask_b in zip(masks, reversed(masks)):
        first_f32 = first.astype(F32) + exchange(first, "shuf", parts, mask_a).astype(F32)
        second_f32 = second.astype(F32) + exchange(second, "shuf", parts, mask_b).astype(F32)
        first, second = first_f32.astype(BF16), second_f32.astype(BF16)
    total = jnp.concatenate([first_f32, second_f32], axis=0)
    grad_uvqk, grad_wout = total[:, : w_uvqk.shape[1]], total[:, w_uvqk.shape[1] :]

    owner_out, owner_grad = pl.pallas_call(
        partial(post_kernel, parts),
        out_shape=[jax.ShapeDtypeStruct((rows, width), BF16)] * 2,
        in_specs=[SMEM] + [VMEM] * (1 + n_rows),
        out_specs=[VMEM] * 2,
        compiler_params=limit,
        name="post",
    )(me, send_order, *returned)
    return (owner_out[None], owner_grad[None], grad_uvqk, grad_wout)


def solution(mesh):
    data, weight = P("group", "shuf", None), P("group", None)
    return jax.shard_map(
        partial(on_device, mesh.shape["group"], mesh.shape["shuf"]),
        mesh=mesh,
        in_specs=(data, data, weight, weight, data, data, data, data),
        out_specs=(data, data, weight, weight),
        check_vma=False,
    )
```

```python
from functools import partial

import jax
import jax.numpy as jnp
from jax import lax
from jax.experimental import pallas as pl
from jax.experimental.pallas import tpu as pltpu
from jax.sharding import PartitionSpec as P

HEADS = 8
norm_eps = 1e-05
F32 = jnp.float32
BF16 = jnp.bfloat16
VMEM = pl.BlockSpec(memory_space=pltpu.VMEM)
SMEM = pl.BlockSpec(memory_space=pltpu.SMEM)
HBM = pl.BlockSpec(memory_space=pltpu.HBM)
NN = (((1,), (0,)), ((), ()))
NT = (((1,), (1,)), ((), ()))
TN = (((0,), (0,)), ((), ()))


def dot(a, b, dims=NN):
    return lax.dot_general(a, b, dims, preferred_element_type=F32)


def sigmoid(values):
    return 0.5 * jnp.tanh(0.5 * values) + 0.5


def normalize(values):
    center = jnp.mean(values, axis=-1, keepdims=True)
    centred = values - center
    variance = jnp.mean(centred * centred, axis=-1, keepdims=True)
    inv_scale = lax.rsqrt(variance + norm_eps)
    return (centred * inv_scale, inv_scale)


def exchange(value, axis, size, mask):
    return lax.ppermute(value, axis, [(i, i ^ mask) for i in range(size)])


def global_row(index, me, chunk):
    place = lax.div(index, chunk)
    return (me ^ place) * chunk + (index - place * chunk)


def looked_up(order, row):
    blocks = order.shape[1]
    block = row.shape[0] // blocks
    at = lax.div(row, block)
    lane = lax.broadcasted_iota(jnp.int32, (row.shape[0], blocks), 1)
    picked = jnp.where(at == lane, order, 0).astype(F32)
    found = jnp.sum(picked, axis=1, keepdims=True).astype(jnp.int32)
    return found * block + (row - at * block)


def send_matrix(order, me, rows, chunk):
    row = lax.broadcasted_iota(jnp.int32, (rows, 1), 0)
    source = looked_up(order, global_row(row, me, chunk))
    lane = lax.broadcasted_iota(jnp.int32, (rows, rows), 1)
    return (source == lane).astype(F32).astype(BF16)


def recv_matrix(order, me, rows, chunk):
    row = lax.broadcasted_iota(jnp.int32, (rows, 1), 0)
    source = looked_up(order, row)
    lane = lax.broadcasted_iota(jnp.int32, (rows, rows), 1)
    return (source == global_row(lane, me, chunk)).astype(F32).astype(BF16)


def stacked(refs, which):
    return jnp.concatenate([ref[which] for ref in refs], axis=0)


def copy_all(moves, sem):
    copies = [pltpu.make_async_copy(a, b, sem.at[n]) for n, (a, b) in enumerate(moves)]
    for copy in copies:
        copy.start()
    return copies


def pre_kernel(parts, send_in, recv_in, lengths_in, prefixes_in, x_in, cot_in, uvqk_in, out_in, *refs):
    w_out, small_out, piece_outs, refs = refs[0], refs[1], refs[2:-13], refs[-13:]
    send_ref, recv_ref, lengths_ref, prefixes_ref, x_ref, cot_ref, w_ref, small_ref, x_sent, cot_sent = refs[:10]
    sem, sent_sem, flat_sem = refs[10:]
    rows = x_ref.shape[0]
    columns = uvqk_in.shape[1]
    copies = copy_all(
        (
            (send_in, send_ref),
            (x_in, x_ref),
            (cot_in, cot_ref),
            (uvqk_in, w_ref.at[:, :columns]),
            (out_in, w_ref.at[:, columns:]),
            (recv_in, recv_ref),
            (lengths_in, lengths_ref),
            (prefixes_in, prefixes_ref),
        ),
        sem,
    )
    copies[0].wait()
    matrix = send_matrix(send_ref[...], lax.axis_index("shuf"), rows, rows // parts)
    step = rows // len(piece_outs)
    sent = []
    for which, (ref, sent_ref) in enumerate(((x_ref, x_sent), (cot_ref, cot_sent))):
        copies[1 + which].wait()
        sent_ref[...] = dot(matrix, ref[...]).astype(BF16)
        sent += copy_all(
            [(sent_ref.at[pl.ds(k * step, step)], out.at[which]) for k, out in enumerate(piece_outs)],
            sent_sem.at[which],
        )
        if which == 0:
            for copy in copies[3:]:
                copy.wait()
            for n, ref in enumerate((recv_ref, lengths_ref, prefixes_ref)):
                small_ref[n : n + 1, : ref.shape[1]] = ref[...]
            sent += copy_all(((w_ref, w_out), (small_ref, small_out)), flat_sem)
    for copy in sent:
        copy.wait()


def plan_kernel(parts, blocks, users, small_ref, w_ref, own_ref, matrix_ref, scale_ref, w_out, own_out):
    rows = matrix_ref.shape[0]
    w_out[...] = w_ref[...]
    own_out[...] = own_ref[...]
    matrix_ref[...] = recv_matrix(small_ref[0:1, :blocks], lax.axis_index("shuf"), rows, rows // parts)
    row = lax.broadcasted_iota(jnp.int32, (rows, 1), 0)
    low = jnp.zeros((rows, 1), jnp.int32)
    high = jnp.zeros((rows, 1), jnp.int32)
    start = jnp.zeros((1, 1), jnp.int32)
    for u in range(users):
        end = start + small_ref[1:2, u : u + 1]
        mine = (row >= start) & (row < end)
        reach = jnp.minimum(end, jnp.maximum(row + 1, start + small_ref[2:3, u : u + 1]))
        low = jnp.where(mine, start, low)
        high = jnp.where(mine, reach, high)
        start = end
    lane = lax.broadcasted_iota(jnp.int32, (rows, rows), 1)
    scale_ref[...] = jnp.where((lane >= low) & (lane < high), 1.0 / rows, 0.0)


def post_kernel(parts, order_ref, *refs):
    back_refs, (out_ref, grad_ref) = refs[:-2], refs[-2:]
    rows = out_ref.shape[0]
    matrix = send_matrix(order_ref[...], lax.axis_index("shuf"), rows, rows // parts)
    for which, ref in enumerate((out_ref, grad_ref)):
        ref[...] = dot(matrix, stacked(back_refs, which), TN).astype(BF16)


def only(value, h, head_width):
    place = lax.div(lax.broadcasted_iota(jnp.int32, value.shape, 1), head_width)
    return jnp.where(place == h, value, jnp.zeros_like(value))


def blocks_of(width):
    head_width = width // HEADS
    per = max(1, 128 // head_width)
    return head_width, per, per * head_width


def partner_order(masks):
    order = [0]
    for mask in reversed(masks):
        order = order + [mask ^ k for k in order]
    return order


def weight_gradient(keep_ref, give_ref, groups, masks, parts):
    group_me = lax.axis_index("group")
    for which, ref in ((0, keep_ref), (1, give_ref)):
        at = 0
        for lhs_ref, rhs in parts:
            shard = lhs_ref.shape[0] // groups
            lhs = jnp.concatenate(
                [
                    lhs_ref[pl.ds(pl.multiple_of((group_me ^ k ^ which) * shard, shard), shard), :]
                    for k in partner_order(masks)
                ],
                axis=0,
            )
            ref[:, at : at + rhs.shape[1]] = dot(lhs, rhs).astype(BF16)
            at += rhs.shape[1]


def forward_kernel(groups, masks, n_rows, places, matrix_ref, scale_ref, *refs):
    row_refs, refs = refs[:n_rows], refs[n_rows:]
    weight_refs, refs = refs[: len(places)], refs[len(places) :]
    (keep_ref, give_ref, out_ref, w_ref, xt_ref, z_ref, inv_ref, cot_ref, act_ref, slope_ref) = refs[:10]
    bend_ref, gmix_ref, gproj_ref, weights_ref, gt_ref, mix_ref = refs[10:]
    width = mix_ref.shape[1]
    shard = width // groups
    group_me = lax.axis_index("group")

    matrix = matrix_ref[...]
    x = dot(matrix, stacked(row_refs, 0))
    cot = dot(matrix, stacked(row_refs, 1)).astype(BF16)
    cot_ref[...] = cot
    z, inv_scale = normalize(x)
    z_ref[...] = z
    inv_ref[...] = inv_scale
    xn = z.astype(BF16)
    xt_ref[...] = xn.T

    for (k, at), ref in zip(places, weight_refs):
        w_ref[pl.ds(pl.multiple_of((group_me ^ k) * shard, shard), shard), at : at + ref.shape[1]] = ref[...]

    for c in range(4):
        cols = slice(c * width, (c + 1) * width)
        projected = dot(xn, w_ref[:, cols])
        s = sigmoid(projected)
        act = projected * s
        act_ref[:, cols] = act.astype(BF16)
        slope_ref[:, cols] = s + act * (1.0 - s)

    scale = scale_ref[...]
    head_width, per, wide = blocks_of(width)
    for g in range(HEADS // per):
        v, q, k = (act_ref[:, c * width + g * wide : c * width + (g + 1) * wide] for c in (1, 2, 3))
        mixed = 0.0
        for h in range(per):
            scores = dot(only(q, h, head_width), k, NT)
            s = sigmoid(scores)
            value = scores * s
            weights = (value * scale).astype(BF16)
            weights_ref[g * per + h] = weights
            bend_ref[g * per + h] = (s + value * (1.0 - s)) * scale
            mixed = mixed + dot(weights, only(v, h, head_width))
        mix_ref[:, g * wide : (g + 1) * wide] = mixed

    normed, mix_inv = normalize(mix_ref[...])
    gate = act_ref[:, :width].astype(F32)
    gated = (normed * gate).astype(BF16)
    gt_ref[...] = gated.T
    w_out = w_ref[:, 4 * width :]
    out_ref[...] = (dot(gated, w_out) + x).astype(BF16)

    g_gated = dot(cot, w_out, NT).astype(BF16).astype(F32)
    g_u = ((g_gated * normed).astype(BF16).astype(F32) * slope_ref[:, :width]).astype(BF16)
    gproj_ref[:, :width] = g_u
    g_normed = g_gated * gate
    g_mixed = (
        mix_inv
        * (
            g_normed
            - jnp.mean(g_normed, axis=-1, keepdims=True)
            - normed * jnp.mean(g_normed * normed, axis=-1, keepdims=True)
        )
    ).astype(BF16)
    gmix_ref[...] = g_mixed
    for g in range(HEADS // per):
        mine = g_mixed[:, g * wide : (g + 1) * wide]
        g_v = 0.0
        for h in range(per):
            g_v = g_v + dot(weights_ref[g * per + h], only(mine, h, head_width), TN)
        at = slice(width + g * wide, width + (g + 1) * wide)
        gproj_ref[:, at] = (g_v.astype(BF16).astype(F32) * slope_ref[:, at]).astype(BF16)
    early = gproj_ref[:, : keep_ref.shape[1] - width]
    weight_gradient(keep_ref, give_ref, groups, masks, ((gt_ref, cot), (xt_ref, early)))


def backward_kernel(groups, masks, n_rows, matrix_ref, *refs):
    (out_ref, w_ref, xt_ref, z_ref, inv_ref, cot_ref, act_ref, slope_ref) = refs[:8]
    bend_ref, gmix_ref, early_ref, keep_ref, give_ref = refs[8:13]
    back_refs, gproj_ref = refs[13:-1], refs[-1]
    rows, width = out_ref.shape
    head_width, per, wide = blocks_of(width)

    gproj_ref[:, : 2 * width] = early_ref[...]
    for g in range(HEADS // per):
        v, q, k = (act_ref[:, c * width + g * wide : c * width + (g + 1) * wide] for c in (1, 2, 3))
        g_mix = gmix_ref[:, g * wide : (g + 1) * wide]
        g_q = g_k = 0.0
        for h in range(per):
            g_weights = dot(only(g_mix, h, head_width), v, NT).astype(BF16).astype(F32)
            g_scores = (g_weights * bend_ref[g * per + h]).astype(BF16)
            g_q = g_q + dot(g_scores, only(k, h, head_width))
            g_k = g_k + dot(g_scores, only(q, h, head_width), TN)
        for c, value in ((2, g_q), (3, g_k)):
            at = slice(c * width + g * wide, c * width + (g + 1) * wide)
            gproj_ref[:, at] = (value.astype(BF16).astype(F32) * slope_ref[:, at]).astype(BF16)

    late = gproj_ref[:, 4 * width - keep_ref.shape[1] :]
    weight_gradient(keep_ref, give_ref, groups, masks, ((xt_ref, late),))

    z = z_ref[...]
    g_xn = dot(gproj_ref[...], w_ref[:, : 4 * width], NT)
    g_x = (
        inv_ref[...]
        * (
            g_xn
            - jnp.mean(g_xn, axis=-1, keepdims=True)
            - z * jnp.mean(g_xn * z, axis=-1, keepdims=True)
        )
        + cot_ref[...].astype(F32)
    ).astype(BF16)
    step = rows // n_rows
    matrix = matrix_ref[...]
    for which, value in ((0, out_ref[...]), (1, g_x)):
        back = dot(matrix, value, TN).astype(BF16)
        for k, ref in enumerate(back_refs):
            ref[which] = back[k * step : (k + 1) * step]


def on_device(groups, parts, inputs, cotangent, w_uvqk, w_out, send_perm, recv_perm, lengths, prefixes):
    rows, width = inputs.shape[1:]
    shard = w_uvqk.shape[0]
    columns = w_uvqk.shape[1] + w_out.shape[1]
    chunk = rows // parts
    whole_tiles = chunk % 16 == 0
    n_rows = parts if whole_tiles else 1
    send_order, recv_order = send_perm[0], recv_perm[0]
    limit = pltpu.CompilerParams(vmem_limit_bytes=24 * 1024 * 1024)
    rows_shape = jax.ShapeDtypeStruct((2, rows // n_rows, width), BF16)

    def swap_rows(own, pieces):
        if not whole_tiles:
            cut = own.reshape(2, parts, chunk, width)
            own, pieces = cut[:, 0], [cut[:, k] for k in range(1, parts)]
        moved = [own] + [exchange(piece, "shuf", parts, k) for k, piece in enumerate(pieces, 1)]
        return moved if whole_tiles else [jnp.concatenate(moved, axis=1)]

    def spec(shape, dtype=BF16):
        return jax.ShapeDtypeStruct(shape, dtype)

    small_shape = (8, 128)
    w_mine, small, own, *outgoing = pl.pallas_call(
        partial(pre_kernel, parts),
        out_shape=[spec((shard, columns)), spec(small_shape, jnp.int32)] + [rows_shape] * n_rows,
        in_specs=[HBM] * 8,
        out_specs=[HBM] * (2 + n_rows),
        scratch_shapes=[
            pltpu.VMEM(send_order.shape, jnp.int32),
            pltpu.VMEM(recv_order.shape, jnp.int32),
            pltpu.VMEM(lengths[0].shape, jnp.int32),
            pltpu.VMEM(prefixes[0].shape, jnp.int32),
            pltpu.VMEM((rows, width), BF16),
            pltpu.VMEM((rows, width), BF16),
            pltpu.VMEM((shard, columns), BF16),
            pltpu.VMEM(small_shape, jnp.int32),
            pltpu.VMEM((rows, width), BF16),
            pltpu.VMEM((rows, width), BF16),
            pltpu.SemaphoreType.DMA((8,)),
            pltpu.SemaphoreType.DMA((2, n_rows)),
            pltpu.SemaphoreType.DMA((2,)),
        ],
        name="pre",
    )(send_order, recv_order, lengths[0], prefixes[0], inputs[0], cotangent[0], w_uvqk, w_out)
    matrix, scale, w_own, own = pl.pallas_call(
        partial(plan_kernel, parts, recv_order.shape[1], lengths.shape[2]),
        out_shape=[spec((rows, rows)), spec((rows, rows), F32), spec((shard, columns)), rows_shape],
        in_specs=[VMEM] * 3,
        out_specs=[VMEM] * 4,
        compiler_params=limit,
        name="plan",
    )(small, w_mine, own)

    chips = [2**j for j in range(1, groups.bit_length() - 1)]
    middle = columns // 2
    pieces = {(k, 0): exchange(w_mine, "group", groups, k) for k in chips}
    near = list(pieces)
    for k in range(2, groups, 2):
        if k not in chips:
            for at, mask in ((0, k & -k), (middle, 2 ** (k.bit_length() - 1))):
                source = pieces.get((k ^ mask, at))
                if (k ^ mask) in chips:
                    source = pieces[k ^ mask, 0][:, at : at + middle]
                pieces[k, at] = exchange(source, "group", groups, mask)
    close = [w_own] + [pieces[place] for place in near]
    arrived = swap_rows(own, outgoing)
    close, arrived[1:2], matrix, scale = lax.optimization_barrier((close, arrived[1:2], matrix, scale))
    pieces.update(zip([(0, 0)] + near, close))
    for (k, at), piece in list(pieces.items()):
        pieces[k ^ 1, at] = exchange(piece, "group", groups, 1)
    places = sorted(pieces)
    shards = [pieces[place] for place in places]

    half = groups // 2 * shard
    early_width = columns // 2
    keep, give, *saved, _ = pl.pallas_call(
        partial(forward_kernel, groups, chips, n_rows, places),
        out_shape=[
            spec((half, early_width)),
            spec((half, early_width)),
            spec((rows, width)),
            spec((width, columns)),
            spec((width, rows)),
            spec((rows, width), F32),
            spec((rows, 1), F32),
            spec((rows, width)),
            spec((rows, 4 * width)),
            spec((rows, 4 * width), F32),
            spec((HEADS, rows, rows), F32),
            spec((rows, width)),
            spec((rows, 2 * width)),
            spec((HEADS, rows, rows)),
        ],
        in_specs=[VMEM] * (2 + n_rows + len(shards)),
        out_specs=[VMEM] * 14,
        scratch_shapes=[pltpu.VMEM((width, rows), BF16), pltpu.VMEM((rows, width), F32)],
        compiler_params=limit,
        name="forward",
    )(matrix, scale, *arrived, *shards)
    taken = exchange(give, "group", groups, 1)
    keep_late, give_late, *returning = pl.pallas_call(
        partial(backward_kernel, groups, chips[::-1], n_rows),
        out_shape=[spec((half, columns - early_width))] * 2 + [rows_shape] * n_rows,
        in_specs=[VMEM] * (1 + len(saved)),
        out_specs=[VMEM] * (2 + n_rows),
        scratch_shapes=[pltpu.VMEM((rows, 4 * width), BF16)],
        compiler_params=limit,
        name="backward",
    )(matrix, *saved)

    far = [2**j for j in range(parts.bit_length() - 1)]

    def add(mine, other):
        return mine.astype(F32) + other.astype(F32)

    def both_cores(mine, other, beside):
        return lax.optimization_barrier((add(mine, other).astype(BF16), beside))

    def over_chips(total, masks, beside=()):
        for n, mask in enumerate(masks):
            middle = total.shape[0] // 2
            other = exchange(total[middle:], "group", groups, mask)
            if n == 0:
                other, beside = lax.optimization_barrier((other, beside))
            total = add(total[:middle], other).astype(BF16)
        return total, beside

    def over_shuf(total, masks, beside=()):
        for mask in masks[:-1]:
            total = add(total, exchange(total, "shuf", parts, mask)).astype(BF16)
        total, beside = lax.optimization_barrier((total, beside))
        return add(total, exchange(total, "shuf", parts, masks[-1])), beside

    taken, give_late = lax.optimization_barrier((taken, give_late))
    taken_late = exchange(give_late, "group", groups, 1)
    late, returning = both_cores(keep_late, taken_late, returning)
    returned = swap_rows(returning[0], returning[1:])
    early, returned[1:2] = over_chips(add(keep, taken).astype(BF16), chips, returned[1:2])
    early, returned = lax.optimization_barrier((early, returned))
    owner = pl.pallas_call(
        partial(post_kernel, parts),
        out_shape=[spec((rows, width))] * 2,
        in_specs=[VMEM] * (1 + n_rows),
        out_specs=[VMEM] * 2,
        compiler_params=limit,
        name="post",
    )(send_order, *returned)
    early, (owner_out, owner_grad) = over_shuf(early, far[::-1], owner)
    late, _ = over_chips(late, chips[::-1])
    late, _ = over_shuf(late, far)
    grad_uvqk = jnp.concatenate([early[:, width:], late], axis=1)
    grad_wout = early[:, :width]
    return (owner_out[None], owner_grad[None], grad_uvqk, grad_wout)


def solution(mesh):
    data, weight = P("group", "shuf", None), P("group", None)
    return jax.shard_map(
        partial(on_device, mesh.shape["group"], mesh.shape["shuf"]),
        mesh=mesh,
        in_specs=(data, data, weight, weight, data, data, data, data),
        out_specs=(data, data, weight, weight),
        check_vma=False,
    )
```

```python
from functools import partial

import jax
import jax.numpy as jnp
from jax import lax
from jax.experimental import pallas as pl
from jax.experimental.pallas import tpu as pltpu
from jax.sharding import PartitionSpec as P

HEADS = 8
norm_eps = 1e-05
F32 = jnp.float32
BF16 = jnp.bfloat16
VMEM = pl.BlockSpec(memory_space=pltpu.VMEM)
SMEM = pl.BlockSpec(memory_space=pltpu.SMEM)
HBM = pl.BlockSpec(memory_space=pltpu.HBM)
NN = (((1,), (0,)), ((), ()))
NT = (((1,), (1,)), ((), ()))
TN = (((0,), (0,)), ((), ()))


def dot(a, b, dims=NN):
    return lax.dot_general(a, b, dims, preferred_element_type=F32)


def sigmoid(values):
    return 0.5 * jnp.tanh(0.5 * values) + 0.5


def normalize(values):
    center = jnp.mean(values, axis=-1, keepdims=True)
    centred = values - center
    variance = jnp.mean(centred * centred, axis=-1, keepdims=True)
    inv_scale = lax.rsqrt(variance + norm_eps)
    return (centred * inv_scale, inv_scale)


def exchange(value, axis, size, mask):
    return lax.ppermute(value, axis, [(i, i ^ mask) for i in range(size)])


def global_row(index, me, chunk):
    place = lax.div(index, chunk)
    return (me ^ place) * chunk + (index - place * chunk)


def looked_up(order, row):
    blocks = order.shape[1]
    block = row.shape[0] // blocks
    at = lax.div(row, block)
    lane = lax.broadcasted_iota(jnp.int32, (row.shape[0], blocks), 1)
    picked = jnp.where(at == lane, order, 0).astype(F32)
    found = jnp.sum(picked, axis=1, keepdims=True).astype(jnp.int32)
    return found * block + (row - at * block)


def send_matrix(order, me, rows, chunk):
    row = lax.broadcasted_iota(jnp.int32, (rows, 1), 0)
    source = looked_up(order, global_row(row, me, chunk))
    lane = lax.broadcasted_iota(jnp.int32, (rows, rows), 1)
    return (source == lane).astype(F32).astype(BF16)


def recv_matrix(order, me, rows, chunk):
    row = lax.broadcasted_iota(jnp.int32, (rows, 1), 0)
    source = looked_up(order, row)
    lane = lax.broadcasted_iota(jnp.int32, (rows, rows), 1)
    return (source == global_row(lane, me, chunk)).astype(F32).astype(BF16)


def stacked(refs, which):
    return jnp.concatenate([ref[which] for ref in refs], axis=0)


def copy_all(moves, sem):
    copies = [pltpu.make_async_copy(a, b, sem.at[n]) for n, (a, b) in enumerate(moves)]
    for copy in copies:
        copy.start()
    return copies


def pre_kernel(parts, send_in, recv_in, lengths_in, prefixes_in, x_in, cot_in, uvqk_in, out_in, *refs):
    w_out, small_out, piece_outs, refs = refs[0], refs[1], refs[2:-13], refs[-13:]
    send_ref, recv_ref, lengths_ref, prefixes_ref, x_ref, cot_ref, w_ref, small_ref, x_sent, cot_sent = refs[:10]
    sem, sent_sem, flat_sem = refs[10:]
    rows = x_ref.shape[0]
    columns = uvqk_in.shape[1]
    copies = copy_all(
        (
            (send_in, send_ref),
            (x_in, x_ref),
            (cot_in, cot_ref),
            (uvqk_in, w_ref.at[:, :columns]),
            (out_in, w_ref.at[:, columns:]),
            (recv_in, recv_ref),
            (lengths_in, lengths_ref),
            (prefixes_in, prefixes_ref),
        ),
        sem,
    )
    copies[0].wait()
    matrix = send_matrix(send_ref[...], lax.axis_index("shuf"), rows, rows // parts)
    step = rows // len(piece_outs)
    sent = []
    for which, (ref, sent_ref) in enumerate(((x_ref, x_sent), (cot_ref, cot_sent))):
        copies[1 + which].wait()
        sent_ref[...] = dot(matrix, ref[...]).astype(BF16)
        sent += copy_all(
            [(sent_ref.at[pl.ds(k * step, step)], out.at[which]) for k, out in enumerate(piece_outs)],
            sent_sem.at[which],
        )
        if which == 0:
            for copy in copies[3:]:
                copy.wait()
            for n, ref in enumerate((recv_ref, lengths_ref, prefixes_ref)):
                small_ref[n : n + 1, : ref.shape[1]] = ref[...]
            sent += copy_all(((w_ref, w_out), (small_ref, small_out)), flat_sem)
    for copy in sent:
        copy.wait()


def plan_kernel(parts, blocks, users, small_ref, w_ref, own_ref, matrix_ref, scale_ref, w_out, own_out):
    rows = matrix_ref.shape[0]
    w_out[...] = w_ref[...]
    own_out[...] = own_ref[...]
    matrix_ref[...] = recv_matrix(small_ref[0:1, :blocks], lax.axis_index("shuf"), rows, rows // parts)
    row = lax.broadcasted_iota(jnp.int32, (rows, 1), 0)
    low = jnp.zeros((rows, 1), jnp.int32)
    high = jnp.zeros((rows, 1), jnp.int32)
    start = jnp.zeros((1, 1), jnp.int32)
    for u in range(users):
        end = start + small_ref[1:2, u : u + 1]
        mine = (row >= start) & (row < end)
        reach = jnp.minimum(end, jnp.maximum(row + 1, start + small_ref[2:3, u : u + 1]))
        low = jnp.where(mine, start, low)
        high = jnp.where(mine, reach, high)
        start = end
    lane = lax.broadcasted_iota(jnp.int32, (rows, rows), 1)
    scale_ref[...] = jnp.where((lane >= low) & (lane < high), 1.0 / rows, 0.0)


def post_kernel(parts, order_ref, *refs):
    back_refs, (out_ref, grad_ref) = refs[:-2], refs[-2:]
    rows = out_ref.shape[0]
    matrix = send_matrix(order_ref[...], lax.axis_index("shuf"), rows, rows // parts)
    for which, ref in enumerate((out_ref, grad_ref)):
        ref[...] = dot(matrix, stacked(back_refs, which), TN).astype(BF16)


def finish_kernel(early_own, early_other, late_own, late_other, uvqk_ref, out_ref):
    rows = early_own.shape[0]
    width = out_ref.shape[1]
    split = early_own.shape[1] - width
    side = lax.axis_index("shuf") & 1
    for place, early, late in ((side, early_own, late_own), (1 - side, early_other, late_other)):
        at = pl.ds(pl.multiple_of(place * rows, rows), rows)
        out_ref[at, :] = early[:, :width].astype(F32)
        uvqk_ref[at, :split] = early[:, width:].astype(F32)
        uvqk_ref[at, split:] = late[...].astype(F32)


def only(value, h, head_width):
    place = lax.div(lax.broadcasted_iota(jnp.int32, value.shape, 1), head_width)
    return jnp.where(place == h, value, jnp.zeros_like(value))


def blocks_of(width):
    head_width = width // HEADS
    per = max(1, 128 // head_width)
    return head_width, per, per * head_width


def partner_order(masks):
    order = [0]
    for mask in reversed(masks):
        order = order + [mask ^ k for k in order]
    return order


def weight_gradient(keep_ref, give_ref, groups, masks, parts):
    group_me = lax.axis_index("group")
    for which, ref in ((0, keep_ref), (1, give_ref)):
        at = 0
        for lhs_ref, rhs in parts:
            shard = lhs_ref.shape[0] // groups
            lhs = jnp.concatenate(
                [
                    lhs_ref[pl.ds(pl.multiple_of((group_me ^ k ^ which) * shard, shard), shard), :]
                    for k in partner_order(masks)
                ],
                axis=0,
            )
            ref[:, at : at + rhs.shape[1]] = dot(lhs, rhs).astype(BF16)
            at += rhs.shape[1]


def forward_kernel(groups, masks, n_rows, places, matrix_ref, scale_ref, *refs):
    row_refs, refs = refs[:n_rows], refs[n_rows:]
    weight_refs, refs = refs[: len(places)], refs[len(places) :]
    (keep_ref, give_ref, out_ref, w_ref, xt_ref, z_ref, inv_ref, cot_ref, act_ref, slope_ref) = refs[:10]
    bend_ref, gmix_ref, gproj_ref, weights_ref, gt_ref, mix_ref = refs[10:]
    width = mix_ref.shape[1]
    shard = width // groups
    group_me = lax.axis_index("group")

    matrix = matrix_ref[...]
    x = dot(matrix, stacked(row_refs, 0))
    cot = dot(matrix, stacked(row_refs, 1)).astype(BF16)
    cot_ref[...] = cot
    z, inv_scale = normalize(x)
    z_ref[...] = z
    inv_ref[...] = inv_scale
    xn = z.astype(BF16)
    xt_ref[...] = xn.T

    for (k, at), ref in zip(places, weight_refs):
        w_ref[pl.ds(pl.multiple_of((group_me ^ k) * shard, shard), shard), at : at + ref.shape[1]] = ref[...]

    for c in range(4):
        cols = slice(c * width, (c + 1) * width)
        projected = dot(xn, w_ref[:, cols])
        s = sigmoid(projected)
        act = projected * s
        act_ref[:, cols] = act.astype(BF16)
        slope_ref[:, cols] = s + act * (1.0 - s)

    scale = scale_ref[...]
    head_width, per, wide = blocks_of(width)
    for g in range(HEADS // per):
        v, q, k = (act_ref[:, c * width + g * wide : c * width + (g + 1) * wide] for c in (1, 2, 3))
        mixed = 0.0
        for h in range(per):
            scores = dot(only(q, h, head_width), k, NT)
            s = sigmoid(scores)
            value = scores * s
            weights = (value * scale).astype(BF16)
            weights_ref[g * per + h] = weights
            bend_ref[g * per + h] = (s + value * (1.0 - s)) * scale
            mixed = mixed + dot(weights, only(v, h, head_width))
        mix_ref[:, g * wide : (g + 1) * wide] = mixed

    normed, mix_inv = normalize(mix_ref[...])
    gate = act_ref[:, :width].astype(F32)
    gated = (normed * gate).astype(BF16)
    gt_ref[...] = gated.T
    w_out = w_ref[:, 4 * width :]
    out_ref[...] = (dot(gated, w_out) + x).astype(BF16)

    g_gated = dot(cot, w_out, NT).astype(BF16).astype(F32)
    g_u = ((g_gated * normed).astype(BF16).astype(F32) * slope_ref[:, :width]).astype(BF16)
    gproj_ref[:, :width] = g_u
    g_normed = g_gated * gate
    g_mixed = (
        mix_inv
        * (
            g_normed
            - jnp.mean(g_normed, axis=-1, keepdims=True)
            - normed * jnp.mean(g_normed * normed, axis=-1, keepdims=True)
        )
    ).astype(BF16)
    gmix_ref[...] = g_mixed
    for g in range(HEADS // per):
        mine = g_mixed[:, g * wide : (g + 1) * wide]
        g_v = 0.0
        for h in range(per):
            g_v = g_v + dot(weights_ref[g * per + h], only(mine, h, head_width), TN)
        at = slice(width + g * wide, width + (g + 1) * wide)
        gproj_ref[:, at] = (g_v.astype(BF16).astype(F32) * slope_ref[:, at]).astype(BF16)
    early = gproj_ref[:, : keep_ref.shape[1] - width]
    weight_gradient(keep_ref, give_ref, groups, masks, ((gt_ref, cot), (xt_ref, early)))


def backward_kernel(groups, masks, n_rows, matrix_ref, *refs):
    (out_ref, w_ref, xt_ref, z_ref, inv_ref, cot_ref, act_ref, slope_ref) = refs[:8]
    bend_ref, gmix_ref, early_ref, keep_ref, give_ref = refs[8:13]
    back_refs, gproj_ref = refs[13:-1], refs[-1]
    rows, width = out_ref.shape
    head_width, per, wide = blocks_of(width)

    gproj_ref[:, : 2 * width] = early_ref[...]
    for g in range(HEADS // per):
        v, q, k = (act_ref[:, c * width + g * wide : c * width + (g + 1) * wide] for c in (1, 2, 3))
        g_mix = gmix_ref[:, g * wide : (g + 1) * wide]
        g_q = g_k = 0.0
        for h in range(per):
            g_weights = dot(only(g_mix, h, head_width), v, NT).astype(BF16).astype(F32)
            g_scores = (g_weights * bend_ref[g * per + h]).astype(BF16)
            g_q = g_q + dot(g_scores, only(k, h, head_width))
            g_k = g_k + dot(g_scores, only(q, h, head_width), TN)
        for c, value in ((2, g_q), (3, g_k)):
            at = slice(c * width + g * wide, c * width + (g + 1) * wide)
            gproj_ref[:, at] = (value.astype(BF16).astype(F32) * slope_ref[:, at]).astype(BF16)

    late = gproj_ref[:, 4 * width - keep_ref.shape[1] :]
    weight_gradient(keep_ref, give_ref, groups, masks, ((xt_ref, late),))

    z = z_ref[...]
    g_xn = dot(gproj_ref[...], w_ref[:, : 4 * width], NT)
    g_x = (
        inv_ref[...]
        * (
            g_xn
            - jnp.mean(g_xn, axis=-1, keepdims=True)
            - z * jnp.mean(g_xn * z, axis=-1, keepdims=True)
        )
        + cot_ref[...].astype(F32)
    ).astype(BF16)
    step = rows // n_rows
    matrix = matrix_ref[...]
    for which, value in ((0, out_ref[...]), (1, g_x)):
        back = dot(matrix, value, TN).astype(BF16)
        for k, ref in enumerate(back_refs):
            ref[which] = back[k * step : (k + 1) * step]


def on_device(groups, parts, inputs, cotangent, w_uvqk, w_out, send_perm, recv_perm, lengths, prefixes):
    rows, width = inputs.shape[1:]
    shard = w_uvqk.shape[0]
    columns = w_uvqk.shape[1] + w_out.shape[1]
    chunk = rows // parts
    whole_tiles = chunk % 16 == 0
    n_rows = parts if whole_tiles else 1
    send_order, recv_order = send_perm[0], recv_perm[0]
    limit = pltpu.CompilerParams(vmem_limit_bytes=24 * 1024 * 1024)
    rows_shape = jax.ShapeDtypeStruct((2, rows // n_rows, width), BF16)

    def swap_rows(own, pieces):
        if not whole_tiles:
            cut = own.reshape(2, parts, chunk, width)
            own, pieces = cut[:, 0], [cut[:, k] for k in range(1, parts)]
        moved = [own] + [exchange(piece, "shuf", parts, k) for k, piece in enumerate(pieces, 1)]
        return moved if whole_tiles else [jnp.concatenate(moved, axis=1)]

    def spec(shape, dtype=BF16):
        return jax.ShapeDtypeStruct(shape, dtype)

    small_shape = (8, 128)
    w_mine, small, own, *outgoing = pl.pallas_call(
        partial(pre_kernel, parts),
        out_shape=[spec((shard, columns)), spec(small_shape, jnp.int32)] + [rows_shape] * n_rows,
        in_specs=[HBM] * 8,
        out_specs=[HBM] * (2 + n_rows),
        scratch_shapes=[
            pltpu.VMEM(send_order.shape, jnp.int32),
            pltpu.VMEM(recv_order.shape, jnp.int32),
            pltpu.VMEM(lengths[0].shape, jnp.int32),
            pltpu.VMEM(prefixes[0].shape, jnp.int32),
            pltpu.VMEM((rows, width), BF16),
            pltpu.VMEM((rows, width), BF16),
            pltpu.VMEM((shard, columns), BF16),
            pltpu.VMEM(small_shape, jnp.int32),
            pltpu.VMEM((rows, width), BF16),
            pltpu.VMEM((rows, width), BF16),
            pltpu.SemaphoreType.DMA((8,)),
            pltpu.SemaphoreType.DMA((2, n_rows)),
            pltpu.SemaphoreType.DMA((2,)),
        ],
        name="pre",
    )(send_order, recv_order, lengths[0], prefixes[0], inputs[0], cotangent[0], w_uvqk, w_out)
    matrix, scale, w_own, own = pl.pallas_call(
        partial(plan_kernel, parts, recv_order.shape[1], lengths.shape[2]),
        out_shape=[spec((rows, rows)), spec((rows, rows), F32), spec((shard, columns)), rows_shape],
        in_specs=[VMEM] * 3,
        out_specs=[VMEM] * 4,
        compiler_params=limit,
        name="plan",
    )(small, w_mine, own)

    chips = [2**j for j in range(1, groups.bit_length() - 1)]
    middle = columns // 2
    pieces = {(k, 0): exchange(w_mine, "group", groups, k) for k in chips}
    near = list(pieces)
    for k in range(2, groups, 2):
        if k not in chips:
            for at, mask in ((0, k & -k), (middle, 2 ** (k.bit_length() - 1))):
                source = pieces.get((k ^ mask, at))
                if (k ^ mask) in chips:
                    source = pieces[k ^ mask, 0][:, at : at + middle]
                pieces[k, at] = exchange(source, "group", groups, mask)
    close = [w_own] + [pieces[place] for place in near]
    arrived = swap_rows(own, outgoing)
    close, arrived[1:2], matrix, scale = lax.optimization_barrier((close, arrived[1:2], matrix, scale))
    distant = [place for place in pieces if place not in near]
    last, arrived[2:] = lax.optimization_barrier(([pieces[place] for place in distant], arrived[2:]))
    pieces.update(zip([(0, 0)] + near + distant, close + last))
    for (k, at), piece in list(pieces.items()):
        pieces[k ^ 1, at] = exchange(piece, "group", groups, 1)
    places = sorted(pieces)
    shards = [pieces[place] for place in places]

    half = groups // 2 * shard
    early_width = 3 * width
    keep, give, *saved, _ = pl.pallas_call(
        partial(forward_kernel, groups, chips, n_rows, places),
        out_shape=[
            spec((half, early_width)),
            spec((half, early_width)),
            spec((rows, width)),
            spec((width, columns)),
            spec((width, rows)),
            spec((rows, width), F32),
            spec((rows, 1), F32),
            spec((rows, width)),
            spec((rows, 4 * width)),
            spec((rows, 4 * width), F32),
            spec((HEADS, rows, rows), F32),
            spec((rows, width)),
            spec((rows, 2 * width)),
            spec((HEADS, rows, rows)),
        ],
        in_specs=[VMEM] * (2 + n_rows + len(shards)),
        out_specs=[VMEM] * 14,
        scratch_shapes=[pltpu.VMEM((width, rows), BF16), pltpu.VMEM((rows, width), F32)],
        compiler_params=limit,
        name="forward",
    )(matrix, scale, *arrived, *shards)
    taken = exchange(give, "group", groups, 1)
    keep_late, give_late, *returning = pl.pallas_call(
        partial(backward_kernel, groups, chips[::-1], n_rows),
        out_shape=[spec((half, columns - early_width))] * 2 + [rows_shape] * n_rows,
        in_specs=[VMEM] * (1 + len(saved)),
        out_specs=[VMEM] * (2 + n_rows),
        scratch_shapes=[pltpu.VMEM((rows, 4 * width), BF16)],
        compiler_params=limit,
        name="backward",
    )(matrix, *saved)

    far = [2**j for j in range(parts.bit_length() - 1)]

    def add(mine, other):
        return mine.astype(F32) + other.astype(F32)

    def both_cores(mine, other, beside):
        return lax.optimization_barrier((add(mine, other).astype(BF16), beside))

    def over_chips(total, masks, beside=()):
        for n, mask in enumerate(masks):
            middle = total.shape[0] // 2
            other = exchange(total[middle:], "group", groups, mask)
            if n == 0:
                other, beside = lax.optimization_barrier((other, beside))
            total = add(total[:middle], other).astype(BF16)
        return total, beside

    side = lax.axis_index("shuf") & 1

    def over_shuf(total):
        middle = shard // 2
        kept = lax.dynamic_slice_in_dim(total, side * middle, middle)
        sent = lax.dynamic_slice_in_dim(total, (1 - side) * middle, middle)
        total = add(kept, exchange(sent, "shuf", parts, 1)).astype(BF16)
        for mask in far[1:]:
            total = add(total, exchange(total, "shuf", parts, mask)).astype(BF16)
        return total, exchange(total, "shuf", parts, 1)

    taken, give_late = lax.optimization_barrier((taken, give_late))
    taken_late = exchange(give_late, "group", groups, 1)
    late, returning = both_cores(keep_late, taken_late, returning)
    returned = swap_rows(returning[0], returning[1:])
    early, returned[1:2] = over_chips(add(keep, taken).astype(BF16), chips, returned[1:2])
    early, returned = lax.optimization_barrier((early, returned))
    owner = pl.pallas_call(
        partial(post_kernel, parts),
        out_shape=[spec((rows, width))] * 2,
        in_specs=[VMEM] * (1 + n_rows),
        out_specs=[VMEM] * 2,
        compiler_params=limit,
        name="post",
    )(send_order, *returned)
    owner_out, owner_grad = owner
    early = over_shuf(early)
    late, _ = over_chips(late, chips[::-1])
    late = over_shuf(late)
    grad_uvqk, grad_wout = pl.pallas_call(
        finish_kernel,
        out_shape=[spec((shard, 4 * width), F32), spec((shard, width), F32)],
        in_specs=[VMEM] * 4,
        out_specs=[VMEM] * 2,
        compiler_params=limit,
        name="finish",
    )(*early, *late)
    return (owner_out[None], owner_grad[None], grad_uvqk, grad_wout)


def solution(mesh):
    data, weight = P("group", "shuf", None), P("group", None)
    return jax.shard_map(
        partial(on_device, mesh.shape["group"], mesh.shape["shuf"]),
        mesh=mesh,
        in_specs=(data, data, weight, weight, data, data, data, data),
        out_specs=(data, data, weight, weight),
        check_vma=False,
    )
```

```python
from functools import partial

import jax
import jax.numpy as jnp
from jax import lax
from jax.experimental import pallas as pl
from jax.experimental.pallas import tpu as pltpu
from jax.sharding import PartitionSpec as P

HEADS = 8
norm_eps = 1e-05
F32 = jnp.float32
BF16 = jnp.bfloat16
VMEM = pl.BlockSpec(memory_space=pltpu.VMEM)
SMEM = pl.BlockSpec(memory_space=pltpu.SMEM)
HBM = pl.BlockSpec(memory_space=pltpu.HBM)
NN = (((1,), (0,)), ((), ()))
NT = (((1,), (1,)), ((), ()))
TN = (((0,), (0,)), ((), ()))


def dot(a, b, dims=NN):
    return lax.dot_general(a, b, dims, preferred_element_type=F32)


def sigmoid(values):
    return 0.5 * jnp.tanh(0.5 * values) + 0.5


def normalize(values):
    center = jnp.mean(values, axis=-1, keepdims=True)
    centred = values - center
    variance = jnp.mean(centred * centred, axis=-1, keepdims=True)
    inv_scale = lax.rsqrt(variance + norm_eps)
    return (centred * inv_scale, inv_scale)


def exchange(value, axis, size, mask):
    return lax.ppermute(value, axis, [(i, i ^ mask) for i in range(size)])


def global_row(index, me, chunk):
    place = lax.div(index, chunk)
    return (me ^ place) * chunk + (index - place * chunk)


def looked_up(order, row):
    blocks = order.shape[1]
    block = row.shape[0] // blocks
    at = lax.div(row, block)
    lane = lax.broadcasted_iota(jnp.int32, (row.shape[0], blocks), 1)
    picked = jnp.where(at == lane, order, 0).astype(F32)
    found = jnp.sum(picked, axis=1, keepdims=True).astype(jnp.int32)
    return found * block + (row - at * block)


def send_matrix(order, me, rows, chunk):
    row = lax.broadcasted_iota(jnp.int32, (rows, 1), 0)
    source = looked_up(order, global_row(row, me, chunk))
    lane = lax.broadcasted_iota(jnp.int32, (rows, rows), 1)
    return (source == lane).astype(F32).astype(BF16)


def recv_matrix(order, me, rows, chunk):
    row = lax.broadcasted_iota(jnp.int32, (rows, 1), 0)
    source = looked_up(order, row)
    lane = lax.broadcasted_iota(jnp.int32, (rows, rows), 1)
    return (source == global_row(lane, me, chunk)).astype(F32).astype(BF16)


def stacked(refs, which):
    return jnp.concatenate([ref[which] for ref in refs], axis=0)


def copy_all(moves, sem):
    copies = [pltpu.make_async_copy(a, b, sem.at[n]) for n, (a, b) in enumerate(moves)]
    for copy in copies:
        copy.start()
    return copies


def pre_kernel(parts, send_in, recv_in, lengths_in, prefixes_in, x_in, cot_in, uvqk_in, out_in, *refs):
    w_out, small_out, piece_outs, refs = refs[0], refs[1], refs[2:-13], refs[-13:]
    send_ref, recv_ref, lengths_ref, prefixes_ref, x_ref, cot_ref, w_ref, small_ref, x_sent, cot_sent = refs[:10]
    sem, sent_sem, flat_sem = refs[10:]
    rows = x_ref.shape[0]
    columns = uvqk_in.shape[1]
    copies = copy_all(
        (
            (send_in, send_ref),
            (x_in, x_ref),
            (cot_in, cot_ref),
            (uvqk_in, w_ref.at[:, :columns]),
            (out_in, w_ref.at[:, columns:]),
            (recv_in, recv_ref),
            (lengths_in, lengths_ref),
            (prefixes_in, prefixes_ref),
        ),
        sem,
    )
    copies[0].wait()
    matrix = send_matrix(send_ref[...], lax.axis_index("shuf"), rows, rows // parts)
    step = rows // len(piece_outs)
    sent = []
    for which, (ref, sent_ref) in enumerate(((x_ref, x_sent), (cot_ref, cot_sent))):
        copies[1 + which].wait()
        sent_ref[...] = dot(matrix, ref[...]).astype(BF16)
        sent += copy_all(
            [(sent_ref.at[pl.ds(k * step, step)], out.at[which]) for k, out in enumerate(piece_outs)],
            sent_sem.at[which],
        )
        if which == 0:
            for copy in copies[3:]:
                copy.wait()
            for n, ref in enumerate((recv_ref, lengths_ref, prefixes_ref)):
                small_ref[n : n + 1, : ref.shape[1]] = ref[...]
            sent += copy_all(((w_ref, w_out), (small_ref, small_out)), flat_sem)
    for copy in sent:
        copy.wait()


def plan_kernel(parts, blocks, users, small_ref, w_ref, own_ref, matrix_ref, scale_ref, w_out, own_out):
    rows = matrix_ref.shape[0]
    w_out[...] = w_ref[...]
    own_out[...] = own_ref[...]
    matrix_ref[...] = recv_matrix(small_ref[0:1, :blocks], lax.axis_index("shuf"), rows, rows // parts)
    row = lax.broadcasted_iota(jnp.int32, (rows, 1), 0)
    low = jnp.zeros((rows, 1), jnp.int32)
    high = jnp.zeros((rows, 1), jnp.int32)
    start = jnp.zeros((1, 1), jnp.int32)
    for u in range(users):
        end = start + small_ref[1:2, u : u + 1]
        mine = (row >= start) & (row < end)
        reach = jnp.minimum(end, jnp.maximum(row + 1, start + small_ref[2:3, u : u + 1]))
        low = jnp.where(mine, start, low)
        high = jnp.where(mine, reach, high)
        start = end
    lane = lax.broadcasted_iota(jnp.int32, (rows, rows), 1)
    scale_ref[...] = jnp.where((lane >= low) & (lane < high), 1.0 / rows, 0.0)


def post_kernel(parts, order_ref, *refs):
    back_refs, (out_ref, grad_ref) = refs[:-2], refs[-2:]
    rows = out_ref.shape[0]
    matrix = send_matrix(order_ref[...], lax.axis_index("shuf"), rows, rows // parts)
    for which, ref in enumerate((out_ref, grad_ref)):
        ref[...] = dot(matrix, stacked(back_refs, which), TN).astype(BF16)


def finish_kernel(early_own, early_other, late_own, late_other, uvqk_ref, out_ref):
    rows = early_own.shape[0]
    width = out_ref.shape[1]
    split = early_own.shape[1] - width
    side = lax.axis_index("shuf") & 1
    for place, early, late in ((side, early_own, late_own), (1 - side, early_other, late_other)):
        at = pl.ds(pl.multiple_of(place * rows, rows), rows)
        out_ref[at, :] = early[:, :width].astype(F32)
        uvqk_ref[at, :split] = early[:, width:].astype(F32)
        uvqk_ref[at, split:] = late[...].astype(F32)


def only(value, h, head_width):
    place = lax.div(lax.broadcasted_iota(jnp.int32, value.shape, 1), head_width)
    return jnp.where(place == h, value, jnp.zeros_like(value))


def blocks_of(width):
    head_width = width // HEADS
    per = max(1, 128 // head_width)
    return head_width, per, per * head_width


def partner_order(masks):
    order = [0]
    for mask in reversed(masks):
        order = order + [mask ^ k for k in order]
    return order


def weight_gradient(keep_ref, give_ref, groups, masks, parts):
    group_me = lax.axis_index("group")
    for which, ref in ((0, keep_ref), (1, give_ref)):
        at = 0
        for lhs_ref, rhs in parts:
            shard = lhs_ref.shape[0] // groups
            lhs = jnp.concatenate(
                [
                    lhs_ref[pl.ds(pl.multiple_of((group_me ^ k ^ which) * shard, shard), shard), :]
                    for k in partner_order(masks)
                ],
                axis=0,
            )
            ref[:, at : at + rhs.shape[1]] = dot(lhs, rhs).astype(BF16)
            at += rhs.shape[1]


def norm_kernel(matrix_ref, *refs):
    row_refs, (x_ref, cot_ref, z_ref, inv_ref, xt_ref) = refs[:-5], refs[-5:]
    matrix = matrix_ref[...]
    x = dot(matrix, stacked(row_refs, 0))
    x_ref[...] = x
    cot_ref[...] = dot(matrix, stacked(row_refs, 1)).astype(BF16)
    z, inv_scale = normalize(x)
    z_ref[...] = z
    inv_ref[...] = inv_scale
    xt_ref[...] = z.astype(BF16).T


def forward_kernel(groups, masks, places, scale_ref, x_ref, cot_ref, z_ref, xt_ref, *refs):
    weight_refs, refs = refs[: len(places)], refs[len(places) :]
    (keep_ref, give_ref, out_ref, w_ref, act_ref, slope_ref) = refs[:6]
    bend_ref, gmix_ref, gproj_ref, weights_ref, gt_ref, mix_ref, ggate_ref = refs[6:]
    width = mix_ref.shape[1]
    shard = width // groups
    group_me = lax.axis_index("group")

    xn = z_ref[...].astype(BF16)
    cot = cot_ref[...]
    for (k, at), ref in zip(places, weight_refs):
        w_ref[pl.ds(pl.multiple_of((group_me ^ k) * shard, shard), shard), at : at + ref.shape[1]] = ref[...]

    for c in range(4):
        cols = slice(c * width, (c + 1) * width)
        projected = dot(xn, w_ref[:, cols])
        s = sigmoid(projected)
        act = projected * s
        act_ref[:, cols] = act.astype(BF16)
        slope_ref[:, cols] = s + act * (1.0 - s)

    w_out = w_ref[:, 4 * width :]
    ggate_ref[...] = dot(cot, w_out, NT).astype(BF16)

    scale = scale_ref[...]
    head_width, per, wide = blocks_of(width)
    for g in range(HEADS // per):
        v, q, k = (act_ref[:, c * width + g * wide : c * width + (g + 1) * wide] for c in (1, 2, 3))
        mixed = 0.0
        for h in range(per):
            scores = dot(only(q, h, head_width), k, NT)
            s = sigmoid(scores)
            value = scores * s
            weights = (value * scale).astype(BF16)
            weights_ref[g * per + h] = weights
            bend_ref[g * per + h] = (s + value * (1.0 - s)) * scale
            mixed = mixed + dot(weights, only(v, h, head_width))
        mix_ref[:, g * wide : (g + 1) * wide] = mixed

    normed, mix_inv = normalize(mix_ref[...])
    gate = act_ref[:, :width].astype(F32)
    gated = (normed * gate).astype(BF16)
    gt_ref[...] = gated.T
    out_ref[...] = (dot(gated, w_out) + x_ref[...]).astype(BF16)

    g_gated = ggate_ref[...].astype(F32)
    g_u = ((g_gated * normed).astype(BF16).astype(F32) * slope_ref[:, :width]).astype(BF16)
    gproj_ref[:, :width] = g_u
    g_normed = g_gated * gate
    g_mixed = (
        mix_inv
        * (
            g_normed
            - jnp.mean(g_normed, axis=-1, keepdims=True)
            - normed * jnp.mean(g_normed * normed, axis=-1, keepdims=True)
        )
    ).astype(BF16)
    gmix_ref[...] = g_mixed
    for g in range(HEADS // per):
        mine = g_mixed[:, g * wide : (g + 1) * wide]
        g_v = 0.0
        for h in range(per):
            g_v = g_v + dot(weights_ref[g * per + h], only(mine, h, head_width), TN)
        at = slice(width + g * wide, width + (g + 1) * wide)
        gproj_ref[:, at] = (g_v.astype(BF16).astype(F32) * slope_ref[:, at]).astype(BF16)
    early = gproj_ref[:, : keep_ref.shape[1] - width]
    weight_gradient(keep_ref, give_ref, groups, masks, ((gt_ref, cot), (xt_ref, early)))


def backward_kernel(
    groups, masks, xt_ref, act_ref, slope_ref, bend_ref, gmix_ref, early_ref, keep_ref, give_ref, gproj_ref
):
    width = gmix_ref.shape[1]
    head_width, per, wide = blocks_of(width)

    gproj_ref[:, : 2 * width] = early_ref[...]
    for g in range(HEADS // per):
        v, q, k = (act_ref[:, c * width + g * wide : c * width + (g + 1) * wide] for c in (1, 2, 3))
        g_mix = gmix_ref[:, g * wide : (g + 1) * wide]
        g_q = g_k = 0.0
        for h in range(per):
            g_weights = dot(only(g_mix, h, head_width), v, NT).astype(BF16).astype(F32)
            g_scores = (g_weights * bend_ref[g * per + h]).astype(BF16)
            g_q = g_q + dot(g_scores, only(k, h, head_width))
            g_k = g_k + dot(g_scores, only(q, h, head_width), TN)
        for c, value in ((2, g_q), (3, g_k)):
            at = slice(c * width + g * wide, c * width + (g + 1) * wide)
            gproj_ref[:, at] = (value.astype(BF16).astype(F32) * slope_ref[:, at]).astype(BF16)

    late = gproj_ref[:, 4 * width - keep_ref.shape[1] :]
    weight_gradient(keep_ref, give_ref, groups, masks, ((xt_ref, late),))


def rows_kernel(matrix_ref, gproj_ref, w_ref, out_ref, z_ref, inv_ref, cot_ref, *back_refs):
    rows, width = out_ref.shape
    z = z_ref[...]
    g_xn = dot(gproj_ref[...], w_ref[:, : 4 * width], NT)
    g_x = (
        inv_ref[...]
        * (
            g_xn
            - jnp.mean(g_xn, axis=-1, keepdims=True)
            - z * jnp.mean(g_xn * z, axis=-1, keepdims=True)
        )
        + cot_ref[...].astype(F32)
    ).astype(BF16)
    step = rows // len(back_refs)
    matrix = matrix_ref[...]
    for which, value in ((0, out_ref[...]), (1, g_x)):
        back = dot(matrix, value, TN).astype(BF16)
        for k, ref in enumerate(back_refs):
            ref[which] = back[k * step : (k + 1) * step]


def on_device(groups, parts, inputs, cotangent, w_uvqk, w_out, send_perm, recv_perm, lengths, prefixes):
    rows, width = inputs.shape[1:]
    shard = w_uvqk.shape[0]
    columns = w_uvqk.shape[1] + w_out.shape[1]
    chunk = rows // parts
    whole_tiles = chunk % 16 == 0
    n_rows = parts if whole_tiles else 1
    send_order, recv_order = send_perm[0], recv_perm[0]
    limit = pltpu.CompilerParams(vmem_limit_bytes=24 * 1024 * 1024)
    rows_shape = jax.ShapeDtypeStruct((2, rows // n_rows, width), BF16)

    def swap_rows(own, pieces):
        if not whole_tiles:
            cut = own.reshape(2, parts, chunk, width)
            own, pieces = cut[:, 0], [cut[:, k] for k in range(1, parts)]
        moved = [own] + [exchange(piece, "shuf", parts, k) for k, piece in enumerate(pieces, 1)]
        return moved if whole_tiles else [jnp.concatenate(moved, axis=1)]

    def spec(shape, dtype=BF16):
        return jax.ShapeDtypeStruct(shape, dtype)

    small_shape = (8, 128)
    w_mine, small, own, *outgoing = pl.pallas_call(
        partial(pre_kernel, parts),
        out_shape=[spec((shard, columns)), spec(small_shape, jnp.int32)] + [rows_shape] * n_rows,
        in_specs=[HBM] * 8,
        out_specs=[HBM] * (2 + n_rows),
        scratch_shapes=[
            pltpu.VMEM(send_order.shape, jnp.int32),
            pltpu.VMEM(recv_order.shape, jnp.int32),
            pltpu.VMEM(lengths[0].shape, jnp.int32),
            pltpu.VMEM(prefixes[0].shape, jnp.int32),
            pltpu.VMEM((rows, width), BF16),
            pltpu.VMEM((rows, width), BF16),
            pltpu.VMEM((shard, columns), BF16),
            pltpu.VMEM(small_shape, jnp.int32),
            pltpu.VMEM((rows, width), BF16),
            pltpu.VMEM((rows, width), BF16),
            pltpu.SemaphoreType.DMA((8,)),
            pltpu.SemaphoreType.DMA((2, n_rows)),
            pltpu.SemaphoreType.DMA((2,)),
        ],
        name="pre",
    )(send_order, recv_order, lengths[0], prefixes[0], inputs[0], cotangent[0], w_uvqk, w_out)
    matrix, scale, w_own, own = pl.pallas_call(
        partial(plan_kernel, parts, recv_order.shape[1], lengths.shape[2]),
        out_shape=[spec((rows, rows)), spec((rows, rows), F32), spec((shard, columns)), rows_shape],
        in_specs=[VMEM] * 3,
        out_specs=[VMEM] * 4,
        compiler_params=limit,
        name="plan",
    )(small, w_mine, own)

    chips = [2**j for j in range(1, groups.bit_length() - 1)]
    middle = columns // 2
    pieces = {(k, 0): exchange(w_mine, "group", groups, k) for k in chips}
    near = list(pieces)
    for k in range(2, groups, 2):
        if k not in chips:
            for at, mask in ((0, k & -k), (middle, 2 ** (k.bit_length() - 1))):
                source = pieces.get((k ^ mask, at))
                if (k ^ mask) in chips:
                    source = pieces[k ^ mask, 0][:, at : at + middle]
                pieces[k, at] = exchange(source, "group", groups, mask)
    close = [w_own] + [pieces[place] for place in near]
    arrived = swap_rows(own, outgoing)
    close, arrived[1:2], matrix, scale = lax.optimization_barrier((close, arrived[1:2], matrix, scale))
    distant = [place for place in pieces if place not in near]
    last, arrived[2:] = lax.optimization_barrier(([pieces[place] for place in distant], arrived[2:]))
    pieces.update(zip([(0, 0)] + near + distant, close + last))
    for (k, at), piece in list(pieces.items()):
        pieces[k ^ 1, at] = exchange(piece, "group", groups, 1)
    places = sorted(pieces)
    shards = [pieces[place] for place in places]

    half = groups // 2 * shard
    early_width = 3 * width
    x, cot, z, inv_scale, xt = pl.pallas_call(
        norm_kernel,
        out_shape=[
            spec((rows, width), F32),
            spec((rows, width)),
            spec((rows, width), F32),
            spec((rows, 1), F32),
            spec((width, rows)),
        ],
        in_specs=[VMEM] * (1 + n_rows),
        out_specs=[VMEM] * 5,
        compiler_params=limit,
        name="norm",
    )(matrix, *arrived)
    keep, give, out, full, act, slope, bend, g_mixed, g_early = pl.pallas_call(
        partial(forward_kernel, groups, chips, places),
        out_shape=[
            spec((half, early_width)),
            spec((half, early_width)),
            spec((rows, width)),
            spec((width, columns)),
            spec((rows, 4 * width)),
            spec((rows, 4 * width), F32),
            spec((HEADS, rows, rows), F32),
            spec((rows, width)),
            spec((rows, 2 * width)),
        ],
        in_specs=[VMEM] * (5 + len(shards)),
        out_specs=[VMEM] * 9,
        scratch_shapes=[
            pltpu.VMEM((HEADS, rows, rows), BF16),
            pltpu.VMEM((width, rows), BF16),
            pltpu.VMEM((rows, width), F32),
            pltpu.VMEM((rows, width), BF16),
        ],
        compiler_params=limit,
        name="forward",
    )(scale, x, cot, z, xt, *shards)
    taken = exchange(give, "group", groups, 1)
    keep_late, give_late, g_proj = pl.pallas_call(
        partial(backward_kernel, groups, chips[::-1]),
        out_shape=[spec((half, columns - early_width))] * 2 + [spec((rows, 4 * width))],
        in_specs=[VMEM] * 6,
        out_specs=[VMEM] * 3,
        compiler_params=limit,
        name="backward",
    )(xt, act, slope, bend, g_mixed, g_early)
    far = [2**j for j in range(parts.bit_length() - 1)]

    def add(mine, other):
        return mine.astype(F32) + other.astype(F32)

    def both_cores(mine, other, beside):
        return lax.optimization_barrier((add(mine, other).astype(BF16), beside))

    def over_chips(total, masks, beside=()):
        for n, mask in enumerate(masks):
            middle = total.shape[0] // 2
            other = exchange(total[middle:], "group", groups, mask)
            if n == 0:
                other, beside = lax.optimization_barrier((other, beside))
            total = add(total[:middle], other).astype(BF16)
        return total, beside

    side = lax.axis_index("shuf") & 1

    def over_shuf(total):
        middle = shard // 2
        kept = lax.dynamic_slice_in_dim(total, side * middle, middle)
        sent = lax.dynamic_slice_in_dim(total, (1 - side) * middle, middle)
        total = add(kept, exchange(sent, "shuf", parts, 1)).astype(BF16)
        for mask in far[1:]:
            total = add(total, exchange(total, "shuf", parts, mask)).astype(BF16)
        return total, exchange(total, "shuf", parts, 1)

    taken, give_late = lax.optimization_barrier((taken, give_late))
    taken_late = exchange(give_late, "group", groups, 1)
    early, g_proj = both_cores(keep, taken, g_proj)
    returning = pl.pallas_call(
        rows_kernel,
        out_shape=[rows_shape] * n_rows,
        in_specs=[VMEM] * 7,
        out_specs=[VMEM] * n_rows,
        compiler_params=limit,
        name="rows",
    )(matrix, g_proj, full, out, z, inv_scale, cot)
    late, returning = both_cores(keep_late, taken_late, returning)
    returned = swap_rows(returning[0], returning[1:])
    early, returned[1:2] = over_chips(early, chips, returned[1:2])
    early, returned = lax.optimization_barrier((early, returned))
    owner = pl.pallas_call(
        partial(post_kernel, parts),
        out_shape=[spec((rows, width))] * 2,
        in_specs=[VMEM] * (1 + n_rows),
        out_specs=[VMEM] * 2,
        compiler_params=limit,
        name="post",
    )(send_order, *returned)
    owner_out, owner_grad = owner
    early = over_shuf(early)
    late, _ = over_chips(late, chips[::-1])
    late = over_shuf(late)
    grad_uvqk, grad_wout = pl.pallas_call(
        finish_kernel,
        out_shape=[spec((shard, 4 * width), F32), spec((shard, width), F32)],
        in_specs=[VMEM] * 4,
        out_specs=[VMEM] * 2,
        compiler_params=limit,
        name="finish",
    )(*early, *late)
    return (owner_out[None], owner_grad[None], grad_uvqk, grad_wout)


def solution(mesh):
    data, weight = P("group", "shuf", None), P("group", None)
    return jax.shard_map(
        partial(on_device, mesh.shape["group"], mesh.shape["shuf"]),
        mesh=mesh,
        in_specs=(data, data, weight, weight, data, data, data, data),
        out_specs=(data, data, weight, weight),
        check_vma=False,
    )
```

```python
from functools import partial

import jax
import jax.numpy as jnp
from jax import lax
from jax.experimental import pallas as pl
from jax.experimental.pallas import tpu as pltpu
from jax.sharding import PartitionSpec as P

HEADS = 8
norm_eps = 1e-05
F32 = jnp.float32
BF16 = jnp.bfloat16
VMEM = pl.BlockSpec(memory_space=pltpu.VMEM)
SMEM = pl.BlockSpec(memory_space=pltpu.SMEM)
HBM = pl.BlockSpec(memory_space=pltpu.HBM)
NN = (((1,), (0,)), ((), ()))
NT = (((1,), (1,)), ((), ()))
TN = (((0,), (0,)), ((), ()))


def dot(a, b, dims=NN):
    return lax.dot_general(a, b, dims, preferred_element_type=F32)


def sigmoid(values):
    return 0.5 * jnp.tanh(0.5 * values) + 0.5


def normalize(values):
    center = jnp.mean(values, axis=-1, keepdims=True)
    centred = values - center
    variance = jnp.mean(centred * centred, axis=-1, keepdims=True)
    inv_scale = lax.rsqrt(variance + norm_eps)
    return (centred * inv_scale, inv_scale)


def exchange(value, axis, size, mask):
    return lax.ppermute(value, axis, [(i, i ^ mask) for i in range(size)])


def global_row(index, me, chunk):
    place = lax.div(index, chunk)
    return (me ^ place) * chunk + (index - place * chunk)


def looked_up(order, row):
    blocks = order.shape[1]
    block = row.shape[0] // blocks
    at = lax.div(row, block)
    lane = lax.broadcasted_iota(jnp.int32, (row.shape[0], blocks), 1)
    picked = jnp.where(at == lane, order, 0).astype(F32)
    found = jnp.sum(picked, axis=1, keepdims=True).astype(jnp.int32)
    return found * block + (row - at * block)


def send_matrix(order, me, rows, chunk):
    row = lax.broadcasted_iota(jnp.int32, (rows, 1), 0)
    source = looked_up(order, global_row(row, me, chunk))
    lane = lax.broadcasted_iota(jnp.int32, (rows, rows), 1)
    return (source == lane).astype(F32).astype(BF16)


def recv_matrix(order, me, rows, chunk):
    row = lax.broadcasted_iota(jnp.int32, (rows, 1), 0)
    source = looked_up(order, row)
    lane = lax.broadcasted_iota(jnp.int32, (rows, rows), 1)
    return (source == global_row(lane, me, chunk)).astype(F32).astype(BF16)


def stacked(refs, which):
    return jnp.concatenate([ref[which] for ref in refs], axis=0)


def copy_all(moves, sem):
    copies = [pltpu.make_async_copy(a, b, sem.at[n]) for n, (a, b) in enumerate(moves)]
    for copy in copies:
        copy.start()
    return copies


def pre_kernel(parts, send_in, recv_in, lengths_in, prefixes_in, x_in, cot_in, uvqk_in, out_in, *refs):
    w_out, small_out, piece_outs, refs = refs[0], refs[1], refs[2:-13], refs[-13:]
    send_ref, recv_ref, lengths_ref, prefixes_ref, x_ref, cot_ref, w_ref, small_ref, x_sent, cot_sent = refs[:10]
    sem, sent_sem, flat_sem = refs[10:]
    rows = x_ref.shape[0]
    columns = uvqk_in.shape[1]
    copies = copy_all(
        (
            (send_in, send_ref),
            (x_in, x_ref),
            (cot_in, cot_ref),
            (uvqk_in, w_ref.at[:, :columns]),
            (out_in, w_ref.at[:, columns:]),
            (recv_in, recv_ref),
            (lengths_in, lengths_ref),
            (prefixes_in, prefixes_ref),
        ),
        sem,
    )
    copies[0].wait()
    matrix = send_matrix(send_ref[...], lax.axis_index("shuf"), rows, rows // parts)
    step = rows // len(piece_outs)
    sent = []
    for which, (ref, sent_ref) in enumerate(((x_ref, x_sent), (cot_ref, cot_sent))):
        copies[1 + which].wait()
        sent_ref[...] = dot(matrix, ref[...]).astype(BF16)
        sent += copy_all(
            [(sent_ref.at[pl.ds(k * step, step)], out.at[which]) for k, out in enumerate(piece_outs)],
            sent_sem.at[which],
        )
        if which == 0:
            for copy in copies[3:]:
                copy.wait()
            for n, ref in enumerate((recv_ref, lengths_ref, prefixes_ref)):
                small_ref[n : n + 1, : ref.shape[1]] = ref[...]
            sent += copy_all(((w_ref, w_out), (small_ref, small_out)), flat_sem)
    for copy in sent:
        copy.wait()


def plan_kernel(parts, blocks, users, small_ref, w_ref, own_ref, matrix_ref, scale_ref, w_out, own_out):
    rows = matrix_ref.shape[0]
    w_out[...] = w_ref[...]
    own_out[...] = own_ref[...]
    matrix_ref[...] = recv_matrix(small_ref[0:1, :blocks], lax.axis_index("shuf"), rows, rows // parts)
    row = lax.broadcasted_iota(jnp.int32, (rows, 1), 0)
    low = jnp.zeros((rows, 1), jnp.int32)
    high = jnp.zeros((rows, 1), jnp.int32)
    start = jnp.zeros((1, 1), jnp.int32)
    for u in range(users):
        end = start + small_ref[1:2, u : u + 1]
        mine = (row >= start) & (row < end)
        reach = jnp.minimum(end, jnp.maximum(row + 1, start + small_ref[2:3, u : u + 1]))
        low = jnp.where(mine, start, low)
        high = jnp.where(mine, reach, high)
        start = end
    lane = lax.broadcasted_iota(jnp.int32, (rows, rows), 1)
    scale_ref[...] = jnp.where((lane >= low) & (lane < high), 1.0 / rows, 0.0)


def post_kernel(parts, order_ref, *refs):
    back_refs, (out_ref, grad_ref) = refs[:-2], refs[-2:]
    rows = out_ref.shape[0]
    matrix = send_matrix(order_ref[...], lax.axis_index("shuf"), rows, rows // parts)
    for which, ref in enumerate((out_ref, grad_ref)):
        ref[...] = dot(matrix, stacked(back_refs, which), TN).astype(BF16)


def finish_kernel(early_own, early_other, late_own, late_other, uvqk_ref, out_ref):
    rows = early_own.shape[0]
    width = out_ref.shape[1]
    split = early_own.shape[1] - width
    side = lax.axis_index("shuf") & 1
    for place, early, late in ((side, early_own, late_own), (1 - side, early_other, late_other)):
        at = pl.ds(pl.multiple_of(place * rows, rows), rows)
        out_ref[at, :] = early[:, :width].astype(F32)
        uvqk_ref[at, :split] = early[:, width:].astype(F32)
        uvqk_ref[at, split:] = late[...].astype(F32)


def only(value, h, head_width):
    place = lax.div(lax.broadcasted_iota(jnp.int32, value.shape, 1), head_width)
    return jnp.where(place == h, value, jnp.zeros_like(value))


def apart(value, per, head_width):
    return jnp.concatenate([only(value, h, head_width) for h in range(per)], axis=0)


def blocks_of(width):
    head_width = width // HEADS
    per = max(1, 128 // head_width)
    return head_width, per, per * head_width


def partner_order(masks):
    order = [0]
    for mask in reversed(masks):
        order = order + [mask ^ k for k in order]
    return order


def weight_gradient(keep_ref, give_ref, groups, masks, parts):
    group_me = lax.axis_index("group")
    for which, ref in ((0, keep_ref), (1, give_ref)):
        at = 0
        for lhs_ref, rhs in parts:
            shard = lhs_ref.shape[0] // groups
            lhs = jnp.concatenate(
                [
                    lhs_ref[pl.ds(pl.multiple_of((group_me ^ k ^ which) * shard, shard), shard), :]
                    for k in partner_order(masks)
                ],
                axis=0,
            )
            ref[:, at : at + rhs.shape[1]] = dot(lhs, rhs).astype(BF16)
            at += rhs.shape[1]


def norm_kernel(matrix_ref, *refs):
    row_refs, (x_ref, cot_ref, z_ref, inv_ref, xt_ref) = refs[:-5], refs[-5:]
    matrix = matrix_ref[...]
    x = dot(matrix, stacked(row_refs, 0))
    x_ref[...] = x
    cot_ref[...] = dot(matrix, stacked(row_refs, 1)).astype(BF16)
    z, inv_scale = normalize(x)
    z_ref[...] = z
    inv_ref[...] = inv_scale
    xt_ref[...] = z.astype(BF16).T


def forward_kernel(groups, masks, places, scale_ref, x_ref, cot_ref, z_ref, xt_ref, *refs):
    weight_refs, refs = refs[: len(places)], refs[len(places) :]
    (keep_ref, give_ref, out_ref, w_ref, act_ref, slope_ref) = refs[:6]
    bend_ref, gmix_ref, gproj_ref, weights_ref, gt_ref, mix_ref, ggate_ref = refs[6:]
    width = mix_ref.shape[1]
    shard = width // groups
    group_me = lax.axis_index("group")

    xn = z_ref[...].astype(BF16)
    cot = cot_ref[...]
    for (k, at), ref in zip(places, weight_refs):
        w_ref[pl.ds(pl.multiple_of((group_me ^ k) * shard, shard), shard), at : at + ref.shape[1]] = ref[...]

    for c in range(4):
        cols = slice(c * width, (c + 1) * width)
        projected = dot(xn, w_ref[:, cols])
        s = sigmoid(projected)
        act = projected * s
        act_ref[:, cols] = act.astype(BF16)
        slope_ref[:, cols] = s + act * (1.0 - s)

    w_out = w_ref[:, 4 * width :]
    ggate_ref[...] = dot(cot, w_out, NT).astype(BF16)

    scale = scale_ref[...]
    head_width, per, wide = blocks_of(width)
    rows = scale.shape[0]
    for g in range(HEADS // per):
        v, q, k = (act_ref[:, c * width + g * wide : c * width + (g + 1) * wide] for c in (1, 2, 3))
        both = dot(apart(q, per, head_width), k, NT)
        heads = []
        for h in range(per):
            scores = both[h * rows : (h + 1) * rows]
            s = sigmoid(scores)
            value = scores * s
            heads.append((value * scale).astype(BF16))
            weights_ref[(g * per + h) * rows : (g * per + h + 1) * rows, :] = heads[h]
            bend_ref[g * per + h] = (s + value * (1.0 - s)) * scale
        mix_ref[:, g * wide : (g + 1) * wide] = dot(jnp.concatenate(heads, axis=1), apart(v, per, head_width))

    normed, mix_inv = normalize(mix_ref[...])
    gate = act_ref[:, :width].astype(F32)
    gated = (normed * gate).astype(BF16)
    gt_ref[...] = gated.T
    out_ref[...] = (dot(gated, w_out) + x_ref[...]).astype(BF16)

    g_gated = ggate_ref[...].astype(F32)
    g_u = ((g_gated * normed).astype(BF16).astype(F32) * slope_ref[:, :width]).astype(BF16)
    gproj_ref[:, :width] = g_u
    g_normed = g_gated * gate
    g_mixed = (
        mix_inv
        * (
            g_normed
            - jnp.mean(g_normed, axis=-1, keepdims=True)
            - normed * jnp.mean(g_normed * normed, axis=-1, keepdims=True)
        )
    ).astype(BF16)
    gmix_ref[...] = g_mixed
    for g in range(HEADS // per):
        mine = apart(g_mixed[:, g * wide : (g + 1) * wide], per, head_width)
        g_v = dot(mine, weights_ref[g * per * rows : (g + 1) * per * rows, :], TN).T
        at = slice(width + g * wide, width + (g + 1) * wide)
        gproj_ref[:, at] = (g_v.astype(BF16).astype(F32) * slope_ref[:, at]).astype(BF16)
    early = gproj_ref[:, : keep_ref.shape[1] - width]
    weight_gradient(keep_ref, give_ref, groups, masks, ((gt_ref, cot), (xt_ref, early)))


def backward_kernel(
    groups, masks, xt_ref, act_ref, slope_ref, bend_ref, gmix_ref, early_ref, keep_ref, give_ref, gproj_ref
):
    width = gmix_ref.shape[1]
    head_width, per, wide = blocks_of(width)

    gproj_ref[:, : 2 * width] = early_ref[...]
    for g in range(HEADS // per):
        v, q, k = (act_ref[:, c * width + g * wide : c * width + (g + 1) * wide] for c in (1, 2, 3))
        g_mix = gmix_ref[:, g * wide : (g + 1) * wide]
        both = dot(apart(g_mix, per, head_width), v, NT).astype(BF16).astype(F32)
        rows = v.shape[0]
        heads = [(both[h * rows : (h + 1) * rows] * bend_ref[g * per + h]).astype(BF16) for h in range(per)]
        g_q = dot(jnp.concatenate(heads, axis=1), apart(k, per, head_width))
        g_k = dot(apart(q, per, head_width), jnp.concatenate(heads, axis=0), TN).T
        for c, value in ((2, g_q), (3, g_k)):
            at = slice(c * width + g * wide, c * width + (g + 1) * wide)
            gproj_ref[:, at] = (value.astype(BF16).astype(F32) * slope_ref[:, at]).astype(BF16)

    late = gproj_ref[:, 4 * width - keep_ref.shape[1] :]
    weight_gradient(keep_ref, give_ref, groups, masks, ((xt_ref, late),))


def rows_kernel(matrix_ref, gproj_ref, w_ref, out_ref, z_ref, inv_ref, cot_ref, *back_refs):
    rows, width = out_ref.shape
    z = z_ref[...]
    g_xn = dot(gproj_ref[...], w_ref[:, : 4 * width], NT)
    g_x = (
        inv_ref[...]
        * (
            g_xn
            - jnp.mean(g_xn, axis=-1, keepdims=True)
            - z * jnp.mean(g_xn * z, axis=-1, keepdims=True)
        )
        + cot_ref[...].astype(F32)
    ).astype(BF16)
    step = rows // len(back_refs)
    matrix = matrix_ref[...]
    for which, value in ((0, out_ref[...]), (1, g_x)):
        back = dot(matrix, value, TN).astype(BF16)
        for k, ref in enumerate(back_refs):
            ref[which] = back[k * step : (k + 1) * step]


def on_device(groups, parts, inputs, cotangent, w_uvqk, w_out, send_perm, recv_perm, lengths, prefixes):
    rows, width = inputs.shape[1:]
    shard = w_uvqk.shape[0]
    columns = w_uvqk.shape[1] + w_out.shape[1]
    chunk = rows // parts
    whole_tiles = chunk % 16 == 0
    n_rows = parts if whole_tiles else 1
    send_order, recv_order = send_perm[0], recv_perm[0]
    limit = pltpu.CompilerParams(vmem_limit_bytes=24 * 1024 * 1024)
    rows_shape = jax.ShapeDtypeStruct((2, rows // n_rows, width), BF16)

    def swap_rows(own, pieces):
        if not whole_tiles:
            cut = own.reshape(2, parts, chunk, width)
            own, pieces = cut[:, 0], [cut[:, k] for k in range(1, parts)]
        moved = [own] + [exchange(piece, "shuf", parts, k) for k, piece in enumerate(pieces, 1)]
        return moved if whole_tiles else [jnp.concatenate(moved, axis=1)]

    def spec(shape, dtype=BF16):
        return jax.ShapeDtypeStruct(shape, dtype)

    small_shape = (8, 128)
    w_mine, small, own, *outgoing = pl.pallas_call(
        partial(pre_kernel, parts),
        out_shape=[spec((shard, columns)), spec(small_shape, jnp.int32)] + [rows_shape] * n_rows,
        in_specs=[HBM] * 8,
        out_specs=[HBM] * (2 + n_rows),
        scratch_shapes=[
            pltpu.VMEM(send_order.shape, jnp.int32),
            pltpu.VMEM(recv_order.shape, jnp.int32),
            pltpu.VMEM(lengths[0].shape, jnp.int32),
            pltpu.VMEM(prefixes[0].shape, jnp.int32),
            pltpu.VMEM((rows, width), BF16),
            pltpu.VMEM((rows, width), BF16),
            pltpu.VMEM((shard, columns), BF16),
            pltpu.VMEM(small_shape, jnp.int32),
            pltpu.VMEM((rows, width), BF16),
            pltpu.VMEM((rows, width), BF16),
            pltpu.SemaphoreType.DMA((8,)),
            pltpu.SemaphoreType.DMA((2, n_rows)),
            pltpu.SemaphoreType.DMA((2,)),
        ],
        name="pre",
    )(send_order, recv_order, lengths[0], prefixes[0], inputs[0], cotangent[0], w_uvqk, w_out)
    matrix, scale, w_own, own = pl.pallas_call(
        partial(plan_kernel, parts, recv_order.shape[1], lengths.shape[2]),
        out_shape=[spec((rows, rows)), spec((rows, rows), F32), spec((shard, columns)), rows_shape],
        in_specs=[VMEM] * 3,
        out_specs=[VMEM] * 4,
        compiler_params=limit,
        name="plan",
    )(small, w_mine, own)

    chips = [2**j for j in range(1, groups.bit_length() - 1)]
    middle = columns // 2
    pieces = {(k, 0): exchange(w_mine, "group", groups, k) for k in chips}
    near = list(pieces)
    for k in range(2, groups, 2):
        if k not in chips:
            for at, mask in ((0, k & -k), (middle, 2 ** (k.bit_length() - 1))):
                source = pieces.get((k ^ mask, at))
                if (k ^ mask) in chips:
                    source = pieces[k ^ mask, 0][:, at : at + middle]
                pieces[k, at] = exchange(source, "group", groups, mask)
    close = [w_own] + [pieces[place] for place in near]
    arrived = swap_rows(own, outgoing)
    close, arrived[1:2], matrix, scale = lax.optimization_barrier((close, arrived[1:2], matrix, scale))
    distant = [place for place in pieces if place not in near]
    last, arrived[2:] = lax.optimization_barrier(([pieces[place] for place in distant], arrived[2:]))
    pieces.update(zip([(0, 0)] + near + distant, close + last))
    for (k, at), piece in list(pieces.items()):
        pieces[k ^ 1, at] = exchange(piece, "group", groups, 1)
    places = sorted(pieces)
    shards = [pieces[place] for place in places]

    half = groups // 2 * shard
    early_width = 3 * width
    x, cot, z, inv_scale, xt = pl.pallas_call(
        norm_kernel,
        out_shape=[
            spec((rows, width), F32),
            spec((rows, width)),
            spec((rows, width), F32),
            spec((rows, 1), F32),
            spec((width, rows)),
        ],
        in_specs=[VMEM] * (1 + n_rows),
        out_specs=[VMEM] * 5,
        compiler_params=limit,
        name="norm",
    )(matrix, *arrived)
    keep, give, out, full, act, slope, bend, g_mixed, g_early = pl.pallas_call(
        partial(forward_kernel, groups, chips, places),
        out_shape=[
            spec((half, early_width)),
            spec((half, early_width)),
            spec((rows, width)),
            spec((width, columns)),
            spec((rows, 4 * width)),
            spec((rows, 4 * width), F32),
            spec((HEADS, rows, rows), F32),
            spec((rows, width)),
            spec((rows, 2 * width)),
        ],
        in_specs=[VMEM] * (5 + len(shards)),
        out_specs=[VMEM] * 9,
        scratch_shapes=[
            pltpu.VMEM((HEADS * rows, rows), BF16),
            pltpu.VMEM((width, rows), BF16),
            pltpu.VMEM((rows, width), F32),
            pltpu.VMEM((rows, width), BF16),
        ],
        compiler_params=limit,
        name="forward",
    )(scale, x, cot, z, xt, *shards)
    taken = exchange(give, "group", groups, 1)
    keep_late, give_late, g_proj = pl.pallas_call(
        partial(backward_kernel, groups, chips[::-1]),
        out_shape=[spec((half, columns - early_width))] * 2 + [spec((rows, 4 * width))],
        in_specs=[VMEM] * 6,
        out_specs=[VMEM] * 3,
        compiler_params=limit,
        name="backward",
    )(xt, act, slope, bend, g_mixed, g_early)
    far = [2**j for j in range(parts.bit_length() - 1)]

    def add(mine, other):
        return mine.astype(F32) + other.astype(F32)

    def both_cores(mine, other, beside):
        return lax.optimization_barrier((add(mine, other).astype(BF16), beside))

    def over_chips(total, masks, beside=()):
        for n, mask in enumerate(masks):
            middle = total.shape[0] // 2
            other = exchange(total[middle:], "group", groups, mask)
            if n == 0:
                other, beside = lax.optimization_barrier((other, beside))
            total = add(total[:middle], other).astype(BF16)
        return total, beside

    side = lax.axis_index("shuf") & 1

    def over_shuf(total):
        middle = shard // 2
        kept = lax.dynamic_slice_in_dim(total, side * middle, middle)
        sent = lax.dynamic_slice_in_dim(total, (1 - side) * middle, middle)
        total = add(kept, exchange(sent, "shuf", parts, 1)).astype(BF16)
        for mask in far[1:]:
            total = add(total, exchange(total, "shuf", parts, mask)).astype(BF16)
        return total, exchange(total, "shuf", parts, 1)

    taken, give_late = lax.optimization_barrier((taken, give_late))
    taken_late = exchange(give_late, "group", groups, 1)
    early, g_proj = both_cores(keep, taken, g_proj)
    returning = pl.pallas_call(
        rows_kernel,
        out_shape=[rows_shape] * n_rows,
        in_specs=[VMEM] * 7,
        out_specs=[VMEM] * n_rows,
        compiler_params=limit,
        name="rows",
    )(matrix, g_proj, full, out, z, inv_scale, cot)
    late, returning = both_cores(keep_late, taken_late, returning)
    returned = swap_rows(returning[0], returning[1:])
    early, returned[1:2] = over_chips(early, chips, returned[1:2])
    early, returned = lax.optimization_barrier((early, returned))
    owner = pl.pallas_call(
        partial(post_kernel, parts),
        out_shape=[spec((rows, width))] * 2,
        in_specs=[VMEM] * (1 + n_rows),
        out_specs=[VMEM] * 2,
        compiler_params=limit,
        name="post",
    )(send_order, *returned)
    owner_out, owner_grad = owner
    early = over_shuf(early)
    late, _ = over_chips(late, chips[::-1])
    late = over_shuf(late)
    grad_uvqk, grad_wout = pl.pallas_call(
        finish_kernel,
        out_shape=[spec((shard, 4 * width), F32), spec((shard, width), F32)],
        in_specs=[VMEM] * 4,
        out_specs=[VMEM] * 2,
        compiler_params=limit,
        name="finish",
    )(*early, *late)
    return (owner_out[None], owner_grad[None], grad_uvqk, grad_wout)


def solution(mesh):
    data, weight = P("group", "shuf", None), P("group", None)
    return jax.shard_map(
        partial(on_device, mesh.shape["group"], mesh.shape["shuf"]),
        mesh=mesh,
        in_specs=(data, data, weight, weight, data, data, data, data),
        out_specs=(data, data, weight, weight),
        check_vma=False,
    )
```

```python
from functools import partial

import jax
import jax.numpy as jnp
from jax import lax
from jax.experimental import pallas as pl
from jax.experimental.pallas import tpu as pltpu
from jax.sharding import PartitionSpec as P

HEADS = 8
norm_eps = 1e-05
F32 = jnp.float32
BF16 = jnp.bfloat16
VMEM = pl.BlockSpec(memory_space=pltpu.VMEM)
SMEM = pl.BlockSpec(memory_space=pltpu.SMEM)
HBM = pl.BlockSpec(memory_space=pltpu.HBM)
NN = (((1,), (0,)), ((), ()))
NT = (((1,), (1,)), ((), ()))
TN = (((0,), (0,)), ((), ()))


def dot(a, b, dims=NN):
    return lax.dot_general(a, b, dims, preferred_element_type=F32)


def sigmoid(values):
    return 0.5 * jnp.tanh(0.5 * values) + 0.5


def normalize(values):
    center = jnp.mean(values, axis=-1, keepdims=True)
    centred = values - center
    variance = jnp.mean(centred * centred, axis=-1, keepdims=True)
    inv_scale = lax.rsqrt(variance + norm_eps)
    return (centred * inv_scale, inv_scale)


def exchange(value, axis, size, mask):
    return lax.ppermute(value, axis, [(i, i ^ mask) for i in range(size)])


def global_row(index, me, chunk):
    place = lax.div(index, chunk)
    return (me ^ place) * chunk + (index - place * chunk)


def looked_up(order, row):
    blocks = order.shape[1]
    block = row.shape[0] // blocks
    at = lax.div(row, block)
    lane = lax.broadcasted_iota(jnp.int32, (row.shape[0], blocks), 1)
    picked = jnp.where(at == lane, order, 0).astype(F32)
    found = jnp.sum(picked, axis=1, keepdims=True).astype(jnp.int32)
    return found * block + (row - at * block)


def send_matrix(order, me, rows, chunk):
    row = lax.broadcasted_iota(jnp.int32, (rows, 1), 0)
    source = looked_up(order, global_row(row, me, chunk))
    lane = lax.broadcasted_iota(jnp.int32, (rows, rows), 1)
    return (source == lane).astype(F32).astype(BF16)


def recv_matrix(order, me, rows, chunk):
    row = lax.broadcasted_iota(jnp.int32, (rows, 1), 0)
    source = looked_up(order, row)
    lane = lax.broadcasted_iota(jnp.int32, (rows, rows), 1)
    return (source == global_row(lane, me, chunk)).astype(F32).astype(BF16)


def stacked(refs, which):
    return jnp.concatenate([ref[which] for ref in refs], axis=0)


def copy_all(moves, sem):
    copies = [pltpu.make_async_copy(a, b, sem.at[n]) for n, (a, b) in enumerate(moves)]
    for copy in copies:
        copy.start()
    return copies


def pre_kernel(parts, send_in, recv_in, lengths_in, prefixes_in, x_in, cot_in, uvqk_in, out_in, *refs):
    w_out, small_out, piece_outs, refs = refs[0], refs[1], refs[2:-13], refs[-13:]
    send_ref, recv_ref, lengths_ref, prefixes_ref, x_ref, cot_ref, w_ref, small_ref, x_sent, cot_sent = refs[:10]
    sem, sent_sem, flat_sem = refs[10:]
    rows = x_ref.shape[0]
    columns = uvqk_in.shape[1]
    copies = copy_all(
        (
            (send_in, send_ref),
            (x_in, x_ref),
            (cot_in, cot_ref),
            (uvqk_in, w_ref.at[:, :columns]),
            (out_in, w_ref.at[:, columns:]),
            (recv_in, recv_ref),
            (lengths_in, lengths_ref),
            (prefixes_in, prefixes_ref),
        ),
        sem,
    )
    copies[0].wait()
    matrix = send_matrix(send_ref[...], lax.axis_index("shuf"), rows, rows // parts)
    step = rows // len(piece_outs)
    sent = []
    for which, (ref, sent_ref) in enumerate(((x_ref, x_sent), (cot_ref, cot_sent))):
        copies[1 + which].wait()
        sent_ref[...] = dot(matrix, ref[...]).astype(BF16)
        sent += copy_all(
            [(sent_ref.at[pl.ds(k * step, step)], out.at[which]) for k, out in enumerate(piece_outs)],
            sent_sem.at[which],
        )
        if which == 0:
            for copy in copies[3:]:
                copy.wait()
            for n, ref in enumerate((recv_ref, lengths_ref, prefixes_ref)):
                small_ref[n : n + 1, : ref.shape[1]] = ref[...]
            sent += copy_all(((w_ref, w_out), (small_ref, small_out)), flat_sem)
    for copy in sent:
        copy.wait()


def plan_kernel(parts, blocks, users, small_ref, w_ref, own_ref, matrix_ref, scale_ref, w_out, own_out):
    rows = matrix_ref.shape[0]
    w_out[...] = w_ref[...]
    own_out[...] = own_ref[...]
    matrix_ref[...] = recv_matrix(small_ref[0:1, :blocks], lax.axis_index("shuf"), rows, rows // parts)
    row = lax.broadcasted_iota(jnp.int32, (rows, 1), 0)
    low = jnp.zeros((rows, 1), jnp.int32)
    high = jnp.zeros((rows, 1), jnp.int32)
    start = jnp.zeros((1, 1), jnp.int32)
    for u in range(users):
        end = start + small_ref[1:2, u : u + 1]
        mine = (row >= start) & (row < end)
        reach = jnp.minimum(end, jnp.maximum(row + 1, start + small_ref[2:3, u : u + 1]))
        low = jnp.where(mine, start, low)
        high = jnp.where(mine, reach, high)
        start = end
    lane = lax.broadcasted_iota(jnp.int32, (rows, rows), 1)
    scale_ref[...] = jnp.where((lane >= low) & (lane < high), 1.0 / rows, 0.0)


def post_kernel(parts, order_ref, *refs):
    back_refs, (out_ref, grad_ref) = refs[:-2], refs[-2:]
    rows = out_ref.shape[0]
    matrix = send_matrix(order_ref[...], lax.axis_index("shuf"), rows, rows // parts)
    for which, ref in enumerate((out_ref, grad_ref)):
        ref[...] = dot(matrix, stacked(back_refs, which), TN).astype(BF16)


def finish_kernel(early_own, early_other, late_own, late_other, uvqk_ref, out_ref):
    rows = early_own.shape[0]
    width = out_ref.shape[1]
    split = early_own.shape[1] - width
    side = lax.axis_index("shuf") & 1
    for place, early, late in ((side, early_own, late_own), (1 - side, early_other, late_other)):
        at = pl.ds(pl.multiple_of(place * rows, rows), rows)
        out_ref[at, :] = early[:, :width].astype(F32)
        uvqk_ref[at, :split] = early[:, width:].astype(F32)
        uvqk_ref[at, split:] = late[...].astype(F32)


def only(value, h, head_width):
    place = lax.div(lax.broadcasted_iota(jnp.int32, value.shape, 1), head_width)
    return jnp.where(place == h, value, jnp.zeros_like(value))


def apart(value, per, head_width):
    return jnp.concatenate([only(value, h, head_width) for h in range(per)], axis=0)


def blocks_of(width):
    head_width = width // HEADS
    per = max(1, 128 // head_width)
    return head_width, per, per * head_width


def partner_order(masks):
    order = [0]
    for mask in reversed(masks):
        order = order + [mask ^ k for k in order]
    return order


def weight_gradient(keep_ref, give_ref, groups, masks, parts):
    group_me = lax.axis_index("group")
    for which, ref in ((0, keep_ref), (1, give_ref)):
        at = 0
        for lhs_ref, rhs in parts:
            shard = lhs_ref.shape[0] // groups
            lhs = jnp.concatenate(
                [
                    lhs_ref[pl.ds(pl.multiple_of((group_me ^ k ^ which) * shard, shard), shard), :]
                    for k in partner_order(masks)
                ],
                axis=0,
            )
            ref[:, at : at + rhs.shape[1]] = dot(lhs, rhs).astype(BF16)
            at += rhs.shape[1]


def norm_kernel(matrix_ref, *refs):
    row_refs, (x_ref, cot_ref, z_ref, inv_ref, xt_ref) = refs[:-5], refs[-5:]
    matrix = matrix_ref[...]
    x = dot(matrix, stacked(row_refs, 0))
    x_ref[...] = x
    cot_ref[...] = dot(matrix, stacked(row_refs, 1)).astype(BF16)
    z, inv_scale = normalize(x)
    z_ref[...] = z
    inv_ref[...] = inv_scale
    xt_ref[...] = z.astype(BF16).T


def forward_kernel(groups, masks, places, scale_ref, x_ref, cot_ref, z_ref, xt_ref, *refs):
    weight_refs, refs = refs[: len(places)], refs[len(places) :]
    (keep_ref, give_ref, out_ref, w_ref, act_ref, slope_ref) = refs[:6]
    bend_ref, gmix_ref, gproj_ref, weights_ref, gt_ref, mix_ref, ggate_ref = refs[6:]
    width = mix_ref.shape[1]
    shard = width // groups
    group_me = lax.axis_index("group")

    xn = z_ref[...].astype(BF16)
    cot = cot_ref[...]
    for (k, at), ref in zip(places, weight_refs):
        w_ref[pl.ds(pl.multiple_of((group_me ^ k) * shard, shard), shard), at : at + ref.shape[1]] = ref[...]

    for c in range(4):
        cols = slice(c * width, (c + 1) * width)
        projected = dot(xn, w_ref[:, cols])
        s = sigmoid(projected)
        act = projected * s
        act_ref[:, cols] = act.astype(BF16)
        slope_ref[:, cols] = s + act * (1.0 - s)

    w_out = w_ref[:, 4 * width :]
    ggate_ref[...] = dot(cot, w_out, NT).astype(BF16)

    scale = scale_ref[...]
    head_width, per, wide = blocks_of(width)
    rows = scale.shape[0]
    for g in range(HEADS // per):
        v, q, k = (act_ref[:, c * width + g * wide : c * width + (g + 1) * wide] for c in (1, 2, 3))
        both = dot(apart(q, per, head_width), k, NT)
        heads = []
        for h in range(per):
            scores = both[h * rows : (h + 1) * rows]
            s = sigmoid(scores)
            value = scores * s
            heads.append((value * scale).astype(BF16))
            weights_ref[(g * per + h) * rows : (g * per + h + 1) * rows, :] = heads[h]
            bend_ref[g * per + h] = (s + value * (1.0 - s)) * scale
        mix_ref[:, g * wide : (g + 1) * wide] = dot(jnp.concatenate(heads, axis=1), apart(v, per, head_width))

    normed, mix_inv = normalize(mix_ref[...])
    gate = act_ref[:, :width].astype(F32)
    gated = (normed * gate).astype(BF16)
    gt_ref[...] = gated.T
    out_ref[...] = (dot(gated, w_out) + x_ref[...]).astype(BF16)

    g_gated = ggate_ref[...].astype(F32)
    g_u = ((g_gated * normed).astype(BF16).astype(F32) * slope_ref[:, :width]).astype(BF16)
    gproj_ref[:, :width] = g_u
    g_normed = g_gated * gate
    g_mixed = (
        mix_inv
        * (
            g_normed
            - jnp.mean(g_normed, axis=-1, keepdims=True)
            - normed * jnp.mean(g_normed * normed, axis=-1, keepdims=True)
        )
    ).astype(BF16)
    gmix_ref[...] = g_mixed
    for g in range(HEADS // per):
        mine = apart(g_mixed[:, g * wide : (g + 1) * wide], per, head_width)
        g_v = dot(mine, weights_ref[g * per * rows : (g + 1) * per * rows, :], TN).T
        at = slice(width + g * wide, width + (g + 1) * wide)
        gproj_ref[:, at] = (g_v.astype(BF16).astype(F32) * slope_ref[:, at]).astype(BF16)
    early = gproj_ref[:, : keep_ref.shape[1] - width]
    weight_gradient(keep_ref, give_ref, groups, masks, ((gt_ref, cot), (xt_ref, early)))


def backward_kernel(
    groups, masks, xt_ref, act_ref, slope_ref, bend_ref, gmix_ref, early_ref, keep_ref, give_ref, gproj_ref
):
    width = gmix_ref.shape[1]
    head_width, per, wide = blocks_of(width)

    gproj_ref[:, : 2 * width] = early_ref[...]
    for g in range(HEADS // per):
        v, q, k = (act_ref[:, c * width + g * wide : c * width + (g + 1) * wide] for c in (1, 2, 3))
        g_mix = gmix_ref[:, g * wide : (g + 1) * wide]
        both = dot(apart(g_mix, per, head_width), v, NT).astype(BF16).astype(F32)
        rows = v.shape[0]
        heads = [(both[h * rows : (h + 1) * rows] * bend_ref[g * per + h]).astype(BF16) for h in range(per)]
        g_q = dot(jnp.concatenate(heads, axis=1), apart(k, per, head_width))
        g_k = dot(apart(q, per, head_width), jnp.concatenate(heads, axis=0), TN).T
        for c, value in ((2, g_q), (3, g_k)):
            at = slice(c * width + g * wide, c * width + (g + 1) * wide)
            gproj_ref[:, at] = (value.astype(BF16).astype(F32) * slope_ref[:, at]).astype(BF16)

    late = gproj_ref[:, 4 * width - keep_ref.shape[1] :]
    weight_gradient(keep_ref, give_ref, groups, masks, ((xt_ref, late),))


def rows_kernel(matrix_ref, gproj_ref, w_ref, out_ref, z_ref, inv_ref, cot_ref, *back_refs):
    rows, width = out_ref.shape
    z = z_ref[...]
    g_xn = dot(gproj_ref[...], w_ref[:, : 4 * width], NT)
    g_x = (
        inv_ref[...]
        * (
            g_xn
            - jnp.mean(g_xn, axis=-1, keepdims=True)
            - z * jnp.mean(g_xn * z, axis=-1, keepdims=True)
        )
        + cot_ref[...].astype(F32)
    ).astype(BF16)
    step = rows // len(back_refs)
    matrix = matrix_ref[...]
    for which, value in ((0, out_ref[...]), (1, g_x)):
        back = dot(matrix, value, TN).astype(BF16)
        for k, ref in enumerate(back_refs):
            ref[which] = back[k * step : (k + 1) * step]


def on_device(groups, parts, inputs, cotangent, w_uvqk, w_out, send_perm, recv_perm, lengths, prefixes):
    rows, width = inputs.shape[1:]
    shard = w_uvqk.shape[0]
    columns = w_uvqk.shape[1] + w_out.shape[1]
    chunk = rows // parts
    whole_tiles = chunk % 16 == 0
    n_rows = parts if whole_tiles else 1
    send_order, recv_order = send_perm[0], recv_perm[0]
    limit = pltpu.CompilerParams(vmem_limit_bytes=24 * 1024 * 1024)
    rows_shape = jax.ShapeDtypeStruct((2, rows // n_rows, width), BF16)

    def swap_rows(own, pieces):
        if not whole_tiles:
            cut = own.reshape(2, parts, chunk, width)
            own, pieces = cut[:, 0], [cut[:, k] for k in range(1, parts)]
        moved = [own] + [exchange(piece, "shuf", parts, k) for k, piece in enumerate(pieces, 1)]
        return moved if whole_tiles else [jnp.concatenate(moved, axis=1)]

    def spec(shape, dtype=BF16):
        return jax.ShapeDtypeStruct(shape, dtype)

    small_shape = (8, 128)
    w_mine, small, own, *outgoing = pl.pallas_call(
        partial(pre_kernel, parts),
        out_shape=[spec((shard, columns)), spec(small_shape, jnp.int32)] + [rows_shape] * n_rows,
        in_specs=[HBM] * 8,
        out_specs=[HBM] * (2 + n_rows),
        scratch_shapes=[
            pltpu.VMEM(send_order.shape, jnp.int32),
            pltpu.VMEM(recv_order.shape, jnp.int32),
            pltpu.VMEM(lengths[0].shape, jnp.int32),
            pltpu.VMEM(prefixes[0].shape, jnp.int32),
            pltpu.VMEM((rows, width), BF16),
            pltpu.VMEM((rows, width), BF16),
            pltpu.VMEM((shard, columns), BF16),
            pltpu.VMEM(small_shape, jnp.int32),
            pltpu.VMEM((rows, width), BF16),
            pltpu.VMEM((rows, width), BF16),
            pltpu.SemaphoreType.DMA((8,)),
            pltpu.SemaphoreType.DMA((2, n_rows)),
            pltpu.SemaphoreType.DMA((2,)),
        ],
        name="pre",
    )(send_order, recv_order, lengths[0], prefixes[0], inputs[0], cotangent[0], w_uvqk, w_out)
    matrix, scale, w_own, own = pl.pallas_call(
        partial(plan_kernel, parts, recv_order.shape[1], lengths.shape[2]),
        out_shape=[spec((rows, rows)), spec((rows, rows), F32), spec((shard, columns)), rows_shape],
        in_specs=[VMEM] * 3,
        out_specs=[VMEM] * 4,
        compiler_params=limit,
        name="plan",
    )(small, w_mine, own)

    chips = [2**j for j in range(1, groups.bit_length() - 1)]
    middle = columns // 2
    pieces = {(k, 0): exchange(w_mine, "group", groups, k) for k in chips}
    near = list(pieces)
    for k in range(2, groups, 2):
        if k not in chips:
            for at, mask in ((0, k & -k), (middle, 2 ** (k.bit_length() - 1))):
                source = pieces.get((k ^ mask, at))
                if (k ^ mask) in chips:
                    source = pieces[k ^ mask, 0][:, at : at + middle]
                pieces[k, at] = exchange(source, "group", groups, mask)
    close = [w_own] + [pieces[place] for place in near]
    arrived = swap_rows(own, outgoing)
    close, arrived[1:2], matrix, scale = lax.optimization_barrier((close, arrived[1:2], matrix, scale))
    distant = [place for place in pieces if place not in near]
    last, arrived[2:] = lax.optimization_barrier(([pieces[place] for place in distant], arrived[2:]))
    pieces.update(zip([(0, 0)] + near + distant, close + last))
    for (k, at), piece in list(pieces.items()):
        pieces[k ^ 1, at] = exchange(piece, "group", groups, 1)
    places = sorted(pieces)
    shards = [pieces[place] for place in places]

    half = groups // 2 * shard
    early_width = 3 * width - 128
    x, cot, z, inv_scale, xt = pl.pallas_call(
        norm_kernel,
        out_shape=[
            spec((rows, width), F32),
            spec((rows, width)),
            spec((rows, width), F32),
            spec((rows, 1), F32),
            spec((width, rows)),
        ],
        in_specs=[VMEM] * (1 + n_rows),
        out_specs=[VMEM] * 5,
        compiler_params=limit,
        name="norm",
    )(matrix, *arrived)
    keep, give, out, full, act, slope, bend, g_mixed, g_early = pl.pallas_call(
        partial(forward_kernel, groups, chips, places),
        out_shape=[
            spec((half, early_width)),
            spec((half, early_width)),
            spec((rows, width)),
            spec((width, columns)),
            spec((rows, 4 * width)),
            spec((rows, 4 * width), F32),
            spec((HEADS, rows, rows), F32),
            spec((rows, width)),
            spec((rows, 2 * width)),
        ],
        in_specs=[VMEM] * (5 + len(shards)),
        out_specs=[VMEM] * 9,
        scratch_shapes=[
            pltpu.VMEM((HEADS * rows, rows), BF16),
            pltpu.VMEM((width, rows), BF16),
            pltpu.VMEM((rows, width), F32),
            pltpu.VMEM((rows, width), BF16),
        ],
        compiler_params=limit,
        name="forward",
    )(scale, x, cot, z, xt, *shards)
    taken = exchange(give, "group", groups, 1)
    keep_late, give_late, g_proj = pl.pallas_call(
        partial(backward_kernel, groups, chips[::-1]),
        out_shape=[spec((half, columns - early_width))] * 2 + [spec((rows, 4 * width))],
        in_specs=[VMEM] * 6,
        out_specs=[VMEM] * 3,
        compiler_params=limit,
        name="backward",
    )(xt, act, slope, bend, g_mixed, g_early)
    far = [2**j for j in range(parts.bit_length() - 1)]

    def add(mine, other):
        return mine.astype(F32) + other.astype(F32)

    def both_cores(mine, other, beside):
        return lax.optimization_barrier((add(mine, other).astype(BF16), beside))

    def over_chips(total, masks, beside=()):
        for n, mask in enumerate(masks):
            middle = total.shape[0] // 2
            other = exchange(total[middle:], "group", groups, mask)
            if n == 0:
                other, beside = lax.optimization_barrier((other, beside))
            total = add(total[:middle], other).astype(BF16)
        return total, beside

    side = lax.axis_index("shuf") & 1

    def over_shuf(total):
        middle = shard // 2
        kept = lax.dynamic_slice_in_dim(total, side * middle, middle)
        sent = lax.dynamic_slice_in_dim(total, (1 - side) * middle, middle)
        total = add(kept, exchange(sent, "shuf", parts, 1)).astype(BF16)
        for mask in far[1:]:
            total = add(total, exchange(total, "shuf", parts, mask)).astype(BF16)
        return total, exchange(total, "shuf", parts, 1)

    taken, give_late = lax.optimization_barrier((taken, give_late))
    taken_late = exchange(give_late, "group", groups, 1)
    early, g_proj = both_cores(keep, taken, g_proj)
    returning = pl.pallas_call(
        rows_kernel,
        out_shape=[rows_shape] * n_rows,
        in_specs=[VMEM] * 7,
        out_specs=[VMEM] * n_rows,
        compiler_params=limit,
        name="rows",
    )(matrix, g_proj, full, out, z, inv_scale, cot)
    late, returning = both_cores(keep_late, taken_late, returning)
    returned = swap_rows(returning[0], returning[1:])
    early, returned[1:2] = over_chips(early, chips, returned[1:2])
    owner = pl.pallas_call(
        partial(post_kernel, parts),
        out_shape=[spec((rows, width))] * 2,
        in_specs=[VMEM] * (1 + n_rows),
        out_specs=[VMEM] * 2,
        compiler_params=limit,
        name="post",
    )(send_order, *returned)
    owner_out, owner_grad = owner
    early, owner_out, owner_grad = lax.optimization_barrier((over_shuf(early), owner_out, owner_grad))
    late, _ = over_chips(late, chips[::-1])
    late = over_shuf(late)
    grad_uvqk, grad_wout = pl.pallas_call(
        finish_kernel,
        out_shape=[spec((shard, 4 * width), F32), spec((shard, width), F32)],
        in_specs=[VMEM] * 4,
        out_specs=[VMEM] * 2,
        compiler_params=limit,
        name="finish",
    )(*early, *late)
    return (owner_out[None], owner_grad[None], grad_uvqk, grad_wout)


def solution(mesh):
    data, weight = P("group", "shuf", None), P("group", None)
    return jax.shard_map(
        partial(on_device, mesh.shape["group"], mesh.shape["shuf"]),
        mesh=mesh,
        in_specs=(data, data, weight, weight, data, data, data, data),
        out_specs=(data, data, weight, weight),
        check_vma=False,
    )
```

```python
from functools import partial

import jax
import jax.numpy as jnp
from jax import lax
from jax.experimental import pallas as pl
from jax.experimental.pallas import tpu as pltpu
from jax.sharding import PartitionSpec as P

HEADS = 8
norm_eps = 1e-05
F32 = jnp.float32
BF16 = jnp.bfloat16
VMEM = pl.BlockSpec(memory_space=pltpu.VMEM)
SMEM = pl.BlockSpec(memory_space=pltpu.SMEM)
HBM = pl.BlockSpec(memory_space=pltpu.HBM)
NN = (((1,), (0,)), ((), ()))
NT = (((1,), (1,)), ((), ()))
TN = (((0,), (0,)), ((), ()))


def dot(a, b, dims=NN):
    return lax.dot_general(a, b, dims, preferred_element_type=F32)


def sigmoid(values):
    return 0.5 * jnp.tanh(0.5 * values) + 0.5


def normalize(values):
    center = jnp.mean(values, axis=-1, keepdims=True)
    centred = values - center
    variance = jnp.mean(centred * centred, axis=-1, keepdims=True)
    inv_scale = lax.rsqrt(variance + norm_eps)
    return (centred * inv_scale, inv_scale)


def exchange(value, axis, size, mask):
    return lax.ppermute(value, axis, [(i, i ^ mask) for i in range(size)])


def global_row(index, me, chunk):
    place = lax.div(index, chunk)
    return (me ^ place) * chunk + (index - place * chunk)


def looked_up(order, row):
    blocks = order.shape[1]
    block = row.shape[0] // blocks
    at = lax.div(row, block)
    lane = lax.broadcasted_iota(jnp.int32, (row.shape[0], blocks), 1)
    picked = jnp.where(at == lane, order, 0).astype(F32)
    found = jnp.sum(picked, axis=1, keepdims=True).astype(jnp.int32)
    return found * block + (row - at * block)


def send_matrix(order, me, rows, chunk):
    row = lax.broadcasted_iota(jnp.int32, (rows, 1), 0)
    source = looked_up(order, global_row(row, me, chunk))
    lane = lax.broadcasted_iota(jnp.int32, (rows, rows), 1)
    return (source == lane).astype(F32).astype(BF16)


def recv_matrix(order, me, rows, chunk):
    row = lax.broadcasted_iota(jnp.int32, (rows, 1), 0)
    source = looked_up(order, row)
    lane = lax.broadcasted_iota(jnp.int32, (rows, rows), 1)
    return (source == global_row(lane, me, chunk)).astype(F32).astype(BF16)


def stacked(refs, which):
    return jnp.concatenate([ref[which] for ref in refs], axis=0)


def copy_all(moves, sem):
    copies = [pltpu.make_async_copy(a, b, sem.at[n]) for n, (a, b) in enumerate(moves)]
    for copy in copies:
        copy.start()
    return copies


def pre_kernel(parts, send_in, recv_in, lengths_in, prefixes_in, x_in, cot_in, uvqk_in, out_in, *refs):
    w_out, small_out, piece_outs, refs = refs[0], refs[1], refs[2:-13], refs[-13:]
    send_ref, recv_ref, lengths_ref, prefixes_ref, x_ref, cot_ref, w_ref, small_ref, x_sent, cot_sent = refs[:10]
    sem, sent_sem, flat_sem = refs[10:]
    rows = x_ref.shape[0]
    columns = uvqk_in.shape[1]
    copies = copy_all(
        (
            (send_in, send_ref),
            (x_in, x_ref),
            (cot_in, cot_ref),
            (uvqk_in, w_ref.at[:, :columns]),
            (out_in, w_ref.at[:, columns:]),
            (recv_in, recv_ref),
            (lengths_in, lengths_ref),
            (prefixes_in, prefixes_ref),
        ),
        sem,
    )
    copies[0].wait()
    matrix = send_matrix(send_ref[...], lax.axis_index("shuf"), rows, rows // parts)
    step = rows // len(piece_outs)
    sent = []
    for which, (ref, sent_ref) in enumerate(((x_ref, x_sent), (cot_ref, cot_sent))):
        copies[1 + which].wait()
        sent_ref[...] = dot(matrix, ref[...]).astype(BF16)
        sent += copy_all(
            [(sent_ref.at[pl.ds(k * step, step)], out.at[which]) for k, out in enumerate(piece_outs)],
            sent_sem.at[which],
        )
        if which == 0:
            for copy in copies[3:]:
                copy.wait()
            for n, ref in enumerate((recv_ref, lengths_ref, prefixes_ref)):
                small_ref[n : n + 1, : ref.shape[1]] = ref[...]
            sent += copy_all(((w_ref, w_out), (small_ref, small_out)), flat_sem)
    for copy in sent:
        copy.wait()


def plan_kernel(parts, blocks, users, small_ref, w_ref, own_ref, matrix_ref, scale_ref, w_out, own_out):
    rows = matrix_ref.shape[0]
    w_out[...] = w_ref[...]
    own_out[...] = own_ref[...]
    matrix_ref[...] = recv_matrix(small_ref[0:1, :blocks], lax.axis_index("shuf"), rows, rows // parts)
    row = lax.broadcasted_iota(jnp.int32, (rows, 1), 0)
    low = jnp.zeros((rows, 1), jnp.int32)
    high = jnp.zeros((rows, 1), jnp.int32)
    start = jnp.zeros((1, 1), jnp.int32)
    for u in range(users):
        end = start + small_ref[1:2, u : u + 1]
        mine = (row >= start) & (row < end)
        reach = jnp.minimum(end, jnp.maximum(row + 1, start + small_ref[2:3, u : u + 1]))
        low = jnp.where(mine, start, low)
        high = jnp.where(mine, reach, high)
        start = end
    lane = lax.broadcasted_iota(jnp.int32, (rows, rows), 1)
    scale_ref[...] = jnp.where((lane >= low) & (lane < high), 1.0 / rows, 0.0)


def post_kernel(parts, order_ref, *refs):
    back_refs, (out_ref, grad_ref) = refs[:-2], refs[-2:]
    rows = out_ref.shape[0]
    matrix = send_matrix(order_ref[...], lax.axis_index("shuf"), rows, rows // parts)
    for which, ref in enumerate((out_ref, grad_ref)):
        ref[...] = dot(matrix, stacked(back_refs, which), TN).astype(BF16)


def finish_kernel(early_own, early_other, late_own, late_other, uvqk_ref, out_ref):
    rows = early_own.shape[0]
    width = out_ref.shape[1]
    split = early_own.shape[1] - width
    side = lax.axis_index("shuf") & 1
    for place, early, late in ((side, early_own, late_own), (1 - side, early_other, late_other)):
        at = pl.ds(pl.multiple_of(place * rows, rows), rows)
        out_ref[at, :] = early[:, :width].astype(F32)
        uvqk_ref[at, :split] = early[:, width:].astype(F32)
        uvqk_ref[at, split:] = late[...].astype(F32)


def only(value, h, head_width):
    place = lax.div(lax.broadcasted_iota(jnp.int32, value.shape, 1), head_width)
    return jnp.where(place == h, value, jnp.zeros_like(value))


def apart(value, per, head_width):
    return jnp.concatenate([only(value, h, head_width) for h in range(per)], axis=0)


def blocks_of(width):
    head_width = width // HEADS
    per = max(1, 128 // head_width)
    return head_width, per, per * head_width


def partner_order(masks):
    order = [0]
    for mask in reversed(masks):
        order = order + [mask ^ k for k in order]
    return order


def weight_gradient(keep_ref, give_ref, groups, masks, parts):
    group_me = lax.axis_index("group")
    for which, ref in ((0, keep_ref), (1, give_ref)):
        at = 0
        for lhs_ref, rhs in parts:
            shard = lhs_ref.shape[0] // groups
            lhs = jnp.concatenate(
                [
                    lhs_ref[pl.ds(pl.multiple_of((group_me ^ k ^ which) * shard, shard), shard), :]
                    for k in partner_order(masks)
                ],
                axis=0,
            )
            ref[:, at : at + rhs.shape[1]] = dot(lhs, rhs).astype(BF16)
            at += rhs.shape[1]


def norm_kernel(matrix_ref, *refs):
    row_refs, (x_ref, cot_ref, z_ref, inv_ref, xt_ref) = refs[:-5], refs[-5:]
    matrix = matrix_ref[...]
    x = dot(matrix, stacked(row_refs, 0))
    x_ref[...] = x
    cot_ref[...] = dot(matrix, stacked(row_refs, 1)).astype(BF16)
    z, inv_scale = normalize(x)
    z_ref[...] = z
    inv_ref[...] = inv_scale
    xt_ref[...] = z.astype(BF16).T


def forward_kernel(groups, masks, places, scale_ref, x_ref, cot_ref, z_ref, xt_ref, *refs):
    weight_refs, refs = refs[: len(places)], refs[len(places) :]
    (keep_ref, give_ref, out_ref, w_ref, act_ref, slope_ref) = refs[:6]
    bend_ref, gmix_ref, gproj_ref, weights_ref, gt_ref, mix_ref, ggate_ref = refs[6:]
    width = mix_ref.shape[1]
    shard = width // groups
    group_me = lax.axis_index("group")

    xn = z_ref[...].astype(BF16)
    cot = cot_ref[...]
    for (k, at), ref in zip(places, weight_refs):
        w_ref[pl.ds(pl.multiple_of((group_me ^ k) * shard, shard), shard), at : at + ref.shape[1]] = ref[...]

    for c in range(4):
        cols = slice(c * width, (c + 1) * width)
        projected = dot(xn, w_ref[:, cols])
        s = sigmoid(projected)
        act = projected * s
        act_ref[:, cols] = act.astype(BF16)
        slope_ref[:, cols] = s + act * (1.0 - s)

    w_out = w_ref[:, 4 * width :]
    ggate_ref[...] = dot(cot, w_out, NT).astype(BF16)

    scale = scale_ref[...]
    head_width, per, wide = blocks_of(width)
    rows = scale.shape[0]
    for g in range(HEADS // per):
        v, q, k = (act_ref[:, c * width + g * wide : c * width + (g + 1) * wide] for c in (1, 2, 3))
        both = dot(apart(q, per, head_width), k, NT)
        heads = []
        for h in range(per):
            scores = both[h * rows : (h + 1) * rows]
            s = sigmoid(scores)
            value = scores * s
            heads.append((value * scale).astype(BF16))
            weights_ref[(g * per + h) * rows : (g * per + h + 1) * rows, :] = heads[h]
            bend_ref[g * per + h] = (s + value * (1.0 - s)) * scale
        mix_ref[:, g * wide : (g + 1) * wide] = dot(jnp.concatenate(heads, axis=1), apart(v, per, head_width))

    normed, mix_inv = normalize(mix_ref[...])
    gate = act_ref[:, :width].astype(F32)
    gated = (normed * gate).astype(BF16)
    gt_ref[...] = gated.T
    out_ref[...] = (dot(gated, w_out) + x_ref[...]).astype(BF16)

    g_gated = ggate_ref[...].astype(F32)
    g_u = ((g_gated * normed).astype(BF16).astype(F32) * slope_ref[:, :width]).astype(BF16)
    gproj_ref[:, :width] = g_u
    g_normed = g_gated * gate
    g_mixed = (
        mix_inv
        * (
            g_normed
            - jnp.mean(g_normed, axis=-1, keepdims=True)
            - normed * jnp.mean(g_normed * normed, axis=-1, keepdims=True)
        )
    ).astype(BF16)
    gmix_ref[...] = g_mixed
    for g in range(HEADS // per):
        mine = apart(g_mixed[:, g * wide : (g + 1) * wide], per, head_width)
        g_v = dot(mine, weights_ref[g * per * rows : (g + 1) * per * rows, :], TN).T
        at = slice(width + g * wide, width + (g + 1) * wide)
        gproj_ref[:, at] = (g_v.astype(BF16).astype(F32) * slope_ref[:, at]).astype(BF16)
    early = gproj_ref[:, : keep_ref.shape[1] - width]
    weight_gradient(keep_ref, give_ref, groups, masks, ((gt_ref, cot), (xt_ref, early)))


def backward_kernel(
    groups, masks, xt_ref, act_ref, slope_ref, bend_ref, gmix_ref, early_ref, keep_ref, give_ref, gproj_ref
):
    width = gmix_ref.shape[1]
    head_width, per, wide = blocks_of(width)

    gproj_ref[:, : 2 * width] = early_ref[...]
    for g in range(HEADS // per):
        v, q, k = (act_ref[:, c * width + g * wide : c * width + (g + 1) * wide] for c in (1, 2, 3))
        g_mix = gmix_ref[:, g * wide : (g + 1) * wide]
        both = dot(apart(g_mix, per, head_width), v, NT).astype(BF16).astype(F32)
        rows = v.shape[0]
        heads = [(both[h * rows : (h + 1) * rows] * bend_ref[g * per + h]).astype(BF16) for h in range(per)]
        g_q = dot(jnp.concatenate(heads, axis=1), apart(k, per, head_width))
        g_k = dot(apart(q, per, head_width), jnp.concatenate(heads, axis=0), TN).T
        for c, value in ((2, g_q), (3, g_k)):
            at = slice(c * width + g * wide, c * width + (g + 1) * wide)
            gproj_ref[:, at] = (value.astype(BF16).astype(F32) * slope_ref[:, at]).astype(BF16)

    late = gproj_ref[:, 4 * width - keep_ref.shape[1] :]
    weight_gradient(keep_ref, give_ref, groups, masks, ((xt_ref, late),))


def rows_kernel(matrix_ref, gproj_ref, w_ref, out_ref, z_ref, inv_ref, cot_ref, *back_refs):
    rows, width = out_ref.shape
    z = z_ref[...]
    g_xn = dot(gproj_ref[...], w_ref[:, : 4 * width], NT)
    g_x = (
        inv_ref[...]
        * (
            g_xn
            - jnp.mean(g_xn, axis=-1, keepdims=True)
            - z * jnp.mean(g_xn * z, axis=-1, keepdims=True)
        )
        + cot_ref[...].astype(F32)
    ).astype(BF16)
    step = rows // len(back_refs)
    matrix = matrix_ref[...]
    for which, value in ((0, out_ref[...]), (1, g_x)):
        back = dot(matrix, value, TN).astype(BF16)
        for k, ref in enumerate(back_refs):
            ref[which] = back[k * step : (k + 1) * step]


def on_device(groups, parts, inputs, cotangent, w_uvqk, w_out, send_perm, recv_perm, lengths, prefixes):
    rows, width = inputs.shape[1:]
    shard = w_uvqk.shape[0]
    columns = w_uvqk.shape[1] + w_out.shape[1]
    chunk = rows // parts
    whole_tiles = chunk % 16 == 0
    n_rows = parts if whole_tiles else 1
    send_order, recv_order = send_perm[0], recv_perm[0]
    limit = pltpu.CompilerParams(vmem_limit_bytes=24 * 1024 * 1024)
    rows_shape = jax.ShapeDtypeStruct((2, rows // n_rows, width), BF16)

    def swap_rows(own, pieces):
        if not whole_tiles:
            cut = own.reshape(2, parts, chunk, width)
            own, pieces = cut[:, 0], [cut[:, k] for k in range(1, parts)]
        moved = [own] + [exchange(piece, "shuf", parts, k) for k, piece in enumerate(pieces, 1)]
        return moved if whole_tiles else [jnp.concatenate(moved, axis=1)]

    def spec(shape, dtype=BF16):
        return jax.ShapeDtypeStruct(shape, dtype)

    small_shape = (8, 128)
    w_mine, small, own, *outgoing = pl.pallas_call(
        partial(pre_kernel, parts),
        out_shape=[spec((shard, columns)), spec(small_shape, jnp.int32)] + [rows_shape] * n_rows,
        in_specs=[HBM] * 8,
        out_specs=[HBM] * (2 + n_rows),
        scratch_shapes=[
            pltpu.VMEM(send_order.shape, jnp.int32),
            pltpu.VMEM(recv_order.shape, jnp.int32),
            pltpu.VMEM(lengths[0].shape, jnp.int32),
            pltpu.VMEM(prefixes[0].shape, jnp.int32),
            pltpu.VMEM((rows, width), BF16),
            pltpu.VMEM((rows, width), BF16),
            pltpu.VMEM((shard, columns), BF16),
            pltpu.VMEM(small_shape, jnp.int32),
            pltpu.VMEM((rows, width), BF16),
            pltpu.VMEM((rows, width), BF16),
            pltpu.SemaphoreType.DMA((8,)),
            pltpu.SemaphoreType.DMA((2, n_rows)),
            pltpu.SemaphoreType.DMA((2,)),
        ],
        name="pre",
    )(send_order, recv_order, lengths[0], prefixes[0], inputs[0], cotangent[0], w_uvqk, w_out)
    matrix, scale, w_own, own = pl.pallas_call(
        partial(plan_kernel, parts, recv_order.shape[1], lengths.shape[2]),
        out_shape=[spec((rows, rows)), spec((rows, rows), F32), spec((shard, columns)), rows_shape],
        in_specs=[VMEM] * 3,
        out_specs=[VMEM] * 4,
        compiler_params=limit,
        name="plan",
    )(small, w_mine, own)

    chips = [2**j for j in range(1, groups.bit_length() - 1)]
    middle = columns // 2
    pieces = {(k, 0): exchange(w_mine, "group", groups, k) for k in chips}
    near = list(pieces)
    for k in range(2, groups, 2):
        if k not in chips:
            for at, mask in ((0, 2 ** (k.bit_length() - 1)), (middle, k & -k)):
                source = pieces.get((k ^ mask, at))
                if (k ^ mask) in chips:
                    source = pieces[k ^ mask, 0][:, at : at + middle]
                pieces[k, at] = exchange(source, "group", groups, mask)
    close = [w_own] + [pieces[place] for place in near]
    arrived = swap_rows(own, outgoing)
    close, arrived[1:2], matrix, scale = lax.optimization_barrier((close, arrived[1:2], matrix, scale))
    distant = [place for place in pieces if place not in near]
    last, arrived[2:] = lax.optimization_barrier(([pieces[place] for place in distant], arrived[2:]))
    pieces.update(zip([(0, 0)] + near + distant, close + last))
    for (k, at), piece in list(pieces.items()):
        pieces[k ^ 1, at] = exchange(piece, "group", groups, 1)
    places = sorted(pieces)
    shards = [pieces[place] for place in places]

    half = groups // 2 * shard
    early_width = 3 * width - 128
    x, cot, z, inv_scale, xt = pl.pallas_call(
        norm_kernel,
        out_shape=[
            spec((rows, width), F32),
            spec((rows, width)),
            spec((rows, width), F32),
            spec((rows, 1), F32),
            spec((width, rows)),
        ],
        in_specs=[VMEM] * (1 + n_rows),
        out_specs=[VMEM] * 5,
        compiler_params=limit,
        name="norm",
    )(matrix, *arrived)
    keep, give, out, full, act, slope, bend, g_mixed, g_early = pl.pallas_call(
        partial(forward_kernel, groups, chips, places),
        out_shape=[
            spec((half, early_width)),
            spec((half, early_width)),
            spec((rows, width)),
            spec((width, columns)),
            spec((rows, 4 * width)),
            spec((rows, 4 * width), F32),
            spec((HEADS, rows, rows), F32),
            spec((rows, width)),
            spec((rows, 2 * width)),
        ],
        in_specs=[VMEM] * (5 + len(shards)),
        out_specs=[VMEM] * 9,
        scratch_shapes=[
            pltpu.VMEM((HEADS * rows, rows), BF16),
            pltpu.VMEM((width, rows), BF16),
            pltpu.VMEM((rows, width), F32),
            pltpu.VMEM((rows, width), BF16),
        ],
        compiler_params=limit,
        name="forward",
    )(scale, x, cot, z, xt, *shards)
    taken = exchange(give, "group", groups, 1)
    keep_late, give_late, g_proj = pl.pallas_call(
        partial(backward_kernel, groups, chips[::-1]),
        out_shape=[spec((half, columns - early_width))] * 2 + [spec((rows, 4 * width))],
        in_specs=[VMEM] * 6,
        out_specs=[VMEM] * 3,
        compiler_params=limit,
        name="backward",
    )(xt, act, slope, bend, g_mixed, g_early)
    far = [2**j for j in range(parts.bit_length() - 1)]

    def add(mine, other):
        return mine.astype(F32) + other.astype(F32)

    def both_cores(mine, other, beside):
        return lax.optimization_barrier((add(mine, other).astype(BF16), beside))

    def over_chips(total, masks, beside=()):
        for n, mask in enumerate(masks):
            middle = total.shape[0] // 2
            other = exchange(total[middle:], "group", groups, mask)
            if n == 0:
                other, beside = lax.optimization_barrier((other, beside))
            total = add(total[:middle], other).astype(BF16)
        return total, beside

    side = lax.axis_index("shuf") & 1

    def over_shuf(total):
        middle = shard // 2
        kept = lax.dynamic_slice_in_dim(total, side * middle, middle)
        sent = lax.dynamic_slice_in_dim(total, (1 - side) * middle, middle)
        total = add(kept, exchange(sent, "shuf", parts, 1)).astype(BF16)
        for mask in far[1:]:
            total = add(total, exchange(total, "shuf", parts, mask)).astype(BF16)
        return total, exchange(total, "shuf", parts, 1)

    taken, give_late = lax.optimization_barrier((taken, give_late))
    taken_late = exchange(give_late, "group", groups, 1)
    early, g_proj = both_cores(keep, taken, g_proj)
    returning = pl.pallas_call(
        rows_kernel,
        out_shape=[rows_shape] * n_rows,
        in_specs=[VMEM] * 7,
        out_specs=[VMEM] * n_rows,
        compiler_params=limit,
        name="rows",
    )(matrix, g_proj, full, out, z, inv_scale, cot)
    late, returning = both_cores(keep_late, taken_late, returning)
    returned = swap_rows(returning[0], returning[1:])
    early, returned[1:2] = over_chips(early, chips, returned[1:2])
    owner = pl.pallas_call(
        partial(post_kernel, parts),
        out_shape=[spec((rows, width))] * 2,
        in_specs=[VMEM] * (1 + n_rows),
        out_specs=[VMEM] * 2,
        compiler_params=limit,
        name="post",
    )(send_order, *returned)
    owner_out, owner_grad = owner
    early, owner_out, owner_grad = lax.optimization_barrier((over_shuf(early), owner_out, owner_grad))
    late, _ = over_chips(late, chips[::-1])
    late = over_shuf(late)
    grad_uvqk, grad_wout = pl.pallas_call(
        finish_kernel,
        out_shape=[spec((shard, 4 * width), F32), spec((shard, width), F32)],
        in_specs=[VMEM] * 4,
        out_specs=[VMEM] * 2,
        compiler_params=limit,
        name="finish",
    )(*early, *late)
    return (owner_out[None], owner_grad[None], grad_uvqk, grad_wout)


def solution(mesh):
    data, weight = P("group", "shuf", None), P("group", None)
    return jax.shard_map(
        partial(on_device, mesh.shape["group"], mesh.shape["shuf"]),
        mesh=mesh,
        in_specs=(data, data, weight, weight, data, data, data, data),
        out_specs=(data, data, weight, weight),
        check_vma=False,
    )
```

```python
from functools import partial

import jax
import jax.numpy as jnp
from jax import lax
from jax.experimental import pallas as pl
from jax.experimental.pallas import tpu as pltpu
from jax.sharding import PartitionSpec as P

HEADS = 8
norm_eps = 1e-05
F32 = jnp.float32
BF16 = jnp.bfloat16
VMEM = pl.BlockSpec(memory_space=pltpu.VMEM)
SMEM = pl.BlockSpec(memory_space=pltpu.SMEM)
HBM = pl.BlockSpec(memory_space=pltpu.HBM)
NN = (((1,), (0,)), ((), ()))
NT = (((1,), (1,)), ((), ()))
TN = (((0,), (0,)), ((), ()))


def dot(a, b, dims=NN):
    return lax.dot_general(a, b, dims, preferred_element_type=F32)


def sigmoid(values):
    return 0.5 * jnp.tanh(0.5 * values) + 0.5


def normalize(values):
    center = jnp.mean(values, axis=-1, keepdims=True)
    centred = values - center
    variance = jnp.mean(centred * centred, axis=-1, keepdims=True)
    inv_scale = lax.rsqrt(variance + norm_eps)
    return (centred * inv_scale, inv_scale)


def exchange(value, axis, size, mask):
    return lax.ppermute(value, axis, [(i, i ^ mask) for i in range(size)])


def global_row(index, me, chunk):
    place = lax.div(index, chunk)
    return (me ^ place) * chunk + (index - place * chunk)


def looked_up(order, row):
    blocks = order.shape[1]
    block = row.shape[0] // blocks
    at = lax.div(row, block)
    lane = lax.broadcasted_iota(jnp.int32, (row.shape[0], blocks), 1)
    picked = jnp.where(at == lane, order, 0).astype(F32)
    found = jnp.sum(picked, axis=1, keepdims=True).astype(jnp.int32)
    return found * block + (row - at * block)


def send_matrix(order, me, rows, chunk):
    row = lax.broadcasted_iota(jnp.int32, (rows, 1), 0)
    source = looked_up(order, global_row(row, me, chunk))
    lane = lax.broadcasted_iota(jnp.int32, (rows, rows), 1)
    return (source == lane).astype(F32).astype(BF16)


def recv_matrix(order, me, rows, chunk):
    row = lax.broadcasted_iota(jnp.int32, (rows, 1), 0)
    source = looked_up(order, row)
    lane = lax.broadcasted_iota(jnp.int32, (rows, rows), 1)
    return (source == global_row(lane, me, chunk)).astype(F32).astype(BF16)


def stacked(refs, which):
    return jnp.concatenate([ref[which] for ref in refs], axis=0)


def copy_all(moves, sem):
    copies = [pltpu.make_async_copy(a, b, sem.at[n]) for n, (a, b) in enumerate(moves)]
    for copy in copies:
        copy.start()
    return copies


def pre_kernel(parts, send_in, recv_in, lengths_in, prefixes_in, x_in, cot_in, uvqk_in, out_in, *refs):
    w_out, small_out, piece_outs, refs = refs[0], refs[1], refs[2:-13], refs[-13:]
    send_ref, recv_ref, lengths_ref, prefixes_ref, x_ref, cot_ref, w_ref, small_ref, x_sent, cot_sent = refs[:10]
    sem, sent_sem, flat_sem = refs[10:]
    rows = x_ref.shape[0]
    columns = uvqk_in.shape[1]
    copies = copy_all(
        (
            (send_in, send_ref),
            (x_in, x_ref),
            (cot_in, cot_ref),
            (uvqk_in, w_ref.at[:, :columns]),
            (out_in, w_ref.at[:, columns:]),
            (recv_in, recv_ref),
            (lengths_in, lengths_ref),
            (prefixes_in, prefixes_ref),
        ),
        sem,
    )
    copies[0].wait()
    matrix = send_matrix(send_ref[...], lax.axis_index("shuf"), rows, rows // parts)
    step = rows // len(piece_outs)
    sent = []
    for which, (ref, sent_ref) in enumerate(((x_ref, x_sent), (cot_ref, cot_sent))):
        copies[1 + which].wait()
        sent_ref[...] = dot(matrix, ref[...]).astype(BF16)
        sent += copy_all(
            [(sent_ref.at[pl.ds(k * step, step)], out.at[which]) for k, out in enumerate(piece_outs)],
            sent_sem.at[which],
        )
        if which == 0:
            for copy in copies[3:]:
                copy.wait()
            for n, ref in enumerate((recv_ref, lengths_ref, prefixes_ref)):
                small_ref[n : n + 1, : ref.shape[1]] = ref[...]
            sent += copy_all(((w_ref, w_out), (small_ref, small_out)), flat_sem)
    for copy in sent:
        copy.wait()


def plan_kernel(parts, blocks, users, small_ref, w_ref, own_ref, matrix_ref, scale_ref, w_out, own_out):
    rows = matrix_ref.shape[0]
    w_out[...] = w_ref[...]
    own_out[...] = own_ref[...]
    matrix_ref[...] = recv_matrix(small_ref[0:1, :blocks], lax.axis_index("shuf"), rows, rows // parts)
    row = lax.broadcasted_iota(jnp.int32, (rows, 1), 0)
    low = jnp.zeros((rows, 1), jnp.int32)
    high = jnp.zeros((rows, 1), jnp.int32)
    start = jnp.zeros((1, 1), jnp.int32)
    for u in range(users):
        end = start + small_ref[1:2, u : u + 1]
        mine = (row >= start) & (row < end)
        reach = jnp.minimum(end, jnp.maximum(row + 1, start + small_ref[2:3, u : u + 1]))
        low = jnp.where(mine, start, low)
        high = jnp.where(mine, reach, high)
        start = end
    lane = lax.broadcasted_iota(jnp.int32, (rows, rows), 1)
    scale_ref[...] = jnp.where((lane >= low) & (lane < high), 1.0 / rows, 0.0)


def post_kernel(parts, order_ref, *refs):
    back_refs, (out_ref, grad_ref) = refs[:-2], refs[-2:]
    rows = out_ref.shape[0]
    matrix = send_matrix(order_ref[...], lax.axis_index("shuf"), rows, rows // parts)
    for which, ref in enumerate((out_ref, grad_ref)):
        ref[...] = dot(matrix, stacked(back_refs, which), TN).astype(BF16)


def finish_kernel(early_own, early_other, late_own, late_other, uvqk_out, wout_out, uvqk_ref, wout_ref, sem):
    rows = early_own.shape[0]
    width = wout_ref.shape[2]
    split = early_own.shape[1] - width
    side = lax.axis_index("shuf") & 1
    copies = []
    for n, place, early, late in ((0, side, early_own, late_own), (1, 1 - side, early_other, late_other)):
        at = pl.ds(pl.multiple_of(place * rows, rows), rows)
        uvqk_ref[n, :, :split] = early[:, width:].astype(F32)
        uvqk_ref[n, :, split:] = late[...].astype(F32)
        wout_ref[n] = early[:, :width].astype(F32)
        copies += copy_all(((uvqk_ref.at[n], uvqk_out.at[at]), (wout_ref.at[n], wout_out.at[at])), sem.at[n])
    for copy in copies:
        copy.wait()


def only(value, h, head_width):
    place = lax.div(lax.broadcasted_iota(jnp.int32, value.shape, 1), head_width)
    return jnp.where(place == h, value, jnp.zeros_like(value))


def apart(value, per, head_width):
    return jnp.concatenate([only(value, h, head_width) for h in range(per)], axis=0)


def blocks_of(width):
    head_width = width // HEADS
    per = max(1, 128 // head_width)
    return head_width, per, per * head_width


def partner_order(masks):
    order = [0]
    for mask in reversed(masks):
        order = order + [mask ^ k for k in order]
    return order


def weight_gradient(keep_ref, give_ref, groups, masks, parts):
    group_me = lax.axis_index("group")
    for which, ref in ((0, keep_ref), (1, give_ref)):
        at = 0
        for lhs_ref, rhs in parts:
            shard = lhs_ref.shape[0] // groups
            lhs = jnp.concatenate(
                [
                    lhs_ref[pl.ds(pl.multiple_of((group_me ^ k ^ which) * shard, shard), shard), :]
                    for k in partner_order(masks)
                ],
                axis=0,
            )
            ref[:, at : at + rhs.shape[1]] = dot(lhs, rhs).astype(BF16)
            at += rhs.shape[1]


def norm_kernel(matrix_ref, *refs):
    row_refs, (x_ref, cot_ref, z_ref, inv_ref, xt_ref) = refs[:-5], refs[-5:]
    matrix = matrix_ref[...]
    x = dot(matrix, stacked(row_refs, 0))
    x_ref[...] = x
    cot_ref[...] = dot(matrix, stacked(row_refs, 1)).astype(BF16)
    z, inv_scale = normalize(x)
    z_ref[...] = z
    inv_ref[...] = inv_scale
    xt_ref[...] = z.astype(BF16).T


def forward_kernel(groups, masks, places, scale_ref, x_ref, cot_ref, z_ref, xt_ref, *refs):
    weight_refs, refs = refs[: len(places)], refs[len(places) :]
    (keep_ref, give_ref, out_ref, w_ref, act_ref, slope_ref) = refs[:6]
    bend_ref, gmix_ref, gproj_ref, weights_ref, gt_ref, mix_ref, ggate_ref = refs[6:]
    width = mix_ref.shape[1]
    shard = width // groups
    group_me = lax.axis_index("group")

    xn = z_ref[...].astype(BF16)
    cot = cot_ref[...]
    for (k, at), ref in zip(places, weight_refs):
        w_ref[pl.ds(pl.multiple_of((group_me ^ k) * shard, shard), shard), at : at + ref.shape[1]] = ref[...]

    for c in range(4):
        cols = slice(c * width, (c + 1) * width)
        projected = dot(xn, w_ref[:, cols])
        s = sigmoid(projected)
        act = projected * s
        act_ref[:, cols] = act.astype(BF16)
        slope_ref[:, cols] = s + act * (1.0 - s)

    w_out = w_ref[:, 4 * width :]
    ggate_ref[...] = dot(cot, w_out, NT).astype(BF16)

    scale = scale_ref[...]
    head_width, per, wide = blocks_of(width)
    rows = scale.shape[0]
    for g in range(HEADS // per):
        v, q, k = (act_ref[:, c * width + g * wide : c * width + (g + 1) * wide] for c in (1, 2, 3))
        both = dot(apart(q, per, head_width), k, NT)
        heads = []
        for h in range(per):
            scores = both[h * rows : (h + 1) * rows]
            s = sigmoid(scores)
            value = scores * s
            heads.append((value * scale).astype(BF16))
            weights_ref[(g * per + h) * rows : (g * per + h + 1) * rows, :] = heads[h]
            bend_ref[g * per + h] = (s + value * (1.0 - s)) * scale
        mix_ref[:, g * wide : (g + 1) * wide] = dot(jnp.concatenate(heads, axis=1), apart(v, per, head_width))

    normed, mix_inv = normalize(mix_ref[...])
    gate = act_ref[:, :width].astype(F32)
    gated = (normed * gate).astype(BF16)
    gt_ref[...] = gated.T
    out_ref[...] = (dot(gated, w_out) + x_ref[...]).astype(BF16)

    g_gated = ggate_ref[...].astype(F32)
    g_u = ((g_gated * normed).astype(BF16).astype(F32) * slope_ref[:, :width]).astype(BF16)
    gproj_ref[:, :width] = g_u
    g_normed = g_gated * gate
    g_mixed = (
        mix_inv
        * (
            g_normed
            - jnp.mean(g_normed, axis=-1, keepdims=True)
            - normed * jnp.mean(g_normed * normed, axis=-1, keepdims=True)
        )
    ).astype(BF16)
    gmix_ref[...] = g_mixed
    for g in range(HEADS // per):
        mine = apart(g_mixed[:, g * wide : (g + 1) * wide], per, head_width)
        g_v = dot(mine, weights_ref[g * per * rows : (g + 1) * per * rows, :], TN).T
        at = slice(width + g * wide, width + (g + 1) * wide)
        gproj_ref[:, at] = (g_v.astype(BF16).astype(F32) * slope_ref[:, at]).astype(BF16)
    early = gproj_ref[:, : keep_ref.shape[1] - width]
    weight_gradient(keep_ref, give_ref, groups, masks, ((gt_ref, cot), (xt_ref, early)))


def backward_kernel(
    groups, masks, xt_ref, act_ref, slope_ref, bend_ref, gmix_ref, early_ref, keep_ref, give_ref, gproj_ref
):
    width = gmix_ref.shape[1]
    head_width, per, wide = blocks_of(width)

    gproj_ref[:, : 2 * width] = early_ref[...]
    for g in range(HEADS // per):
        v, q, k = (act_ref[:, c * width + g * wide : c * width + (g + 1) * wide] for c in (1, 2, 3))
        g_mix = gmix_ref[:, g * wide : (g + 1) * wide]
        both = dot(apart(g_mix, per, head_width), v, NT).astype(BF16).astype(F32)
        rows = v.shape[0]
        heads = [(both[h * rows : (h + 1) * rows] * bend_ref[g * per + h]).astype(BF16) for h in range(per)]
        g_q = dot(jnp.concatenate(heads, axis=1), apart(k, per, head_width))
        g_k = dot(apart(q, per, head_width), jnp.concatenate(heads, axis=0), TN).T
        for c, value in ((2, g_q), (3, g_k)):
            at = slice(c * width + g * wide, c * width + (g + 1) * wide)
            gproj_ref[:, at] = (value.astype(BF16).astype(F32) * slope_ref[:, at]).astype(BF16)

    late = gproj_ref[:, 4 * width - keep_ref.shape[1] :]
    weight_gradient(keep_ref, give_ref, groups, masks, ((xt_ref, late),))


def rows_kernel(matrix_ref, gproj_ref, w_ref, out_ref, z_ref, inv_ref, cot_ref, *back_refs):
    rows, width = out_ref.shape
    z = z_ref[...]
    g_xn = dot(gproj_ref[...], w_ref[:, : 4 * width], NT)
    g_x = (
        inv_ref[...]
        * (
            g_xn
            - jnp.mean(g_xn, axis=-1, keepdims=True)
            - z * jnp.mean(g_xn * z, axis=-1, keepdims=True)
        )
        + cot_ref[...].astype(F32)
    ).astype(BF16)
    step = rows // len(back_refs)
    matrix = matrix_ref[...]
    for which, value in ((0, out_ref[...]), (1, g_x)):
        back = dot(matrix, value, TN).astype(BF16)
        for k, ref in enumerate(back_refs):
            ref[which] = back[k * step : (k + 1) * step]


def on_device(groups, parts, inputs, cotangent, w_uvqk, w_out, send_perm, recv_perm, lengths, prefixes):
    rows, width = inputs.shape[1:]
    shard = w_uvqk.shape[0]
    columns = w_uvqk.shape[1] + w_out.shape[1]
    chunk = rows // parts
    whole_tiles = chunk % 16 == 0
    n_rows = parts if whole_tiles else 1
    send_order, recv_order = send_perm[0], recv_perm[0]
    limit = pltpu.CompilerParams(vmem_limit_bytes=24 * 1024 * 1024)
    rows_shape = jax.ShapeDtypeStruct((2, rows // n_rows, width), BF16)

    def swap_rows(own, pieces):
        if not whole_tiles:
            cut = own.reshape(2, parts, chunk, width)
            own, pieces = cut[:, 0], [cut[:, k] for k in range(1, parts)]
        moved = [own] + [exchange(piece, "shuf", parts, k) for k, piece in enumerate(pieces, 1)]
        return moved if whole_tiles else [jnp.concatenate(moved, axis=1)]

    def spec(shape, dtype=BF16):
        return jax.ShapeDtypeStruct(shape, dtype)

    small_shape = (8, 128)
    w_mine, small, own, *outgoing = pl.pallas_call(
        partial(pre_kernel, parts),
        out_shape=[spec((shard, columns)), spec(small_shape, jnp.int32)] + [rows_shape] * n_rows,
        in_specs=[HBM] * 8,
        out_specs=[HBM] * (2 + n_rows),
        scratch_shapes=[
            pltpu.VMEM(send_order.shape, jnp.int32),
            pltpu.VMEM(recv_order.shape, jnp.int32),
            pltpu.VMEM(lengths[0].shape, jnp.int32),
            pltpu.VMEM(prefixes[0].shape, jnp.int32),
            pltpu.VMEM((rows, width), BF16),
            pltpu.VMEM((rows, width), BF16),
            pltpu.VMEM((shard, columns), BF16),
            pltpu.VMEM(small_shape, jnp.int32),
            pltpu.VMEM((rows, width), BF16),
            pltpu.VMEM((rows, width), BF16),
            pltpu.SemaphoreType.DMA((8,)),
            pltpu.SemaphoreType.DMA((2, n_rows)),
            pltpu.SemaphoreType.DMA((2,)),
        ],
        name="pre",
    )(send_order, recv_order, lengths[0], prefixes[0], inputs[0], cotangent[0], w_uvqk, w_out)
    matrix, scale, w_own, own = pl.pallas_call(
        partial(plan_kernel, parts, recv_order.shape[1], lengths.shape[2]),
        out_shape=[spec((rows, rows)), spec((rows, rows), F32), spec((shard, columns)), rows_shape],
        in_specs=[VMEM] * 3,
        out_specs=[VMEM] * 4,
        compiler_params=limit,
        name="plan",
    )(small, w_mine, own)

    chips = [2**j for j in range(1, groups.bit_length() - 1)]
    middle = columns // 2
    pieces = {(k, 0): exchange(w_mine, "group", groups, k) for k in chips}
    near = list(pieces)
    for k in range(2, groups, 2):
        if k not in chips:
            for at, mask in ((0, 2 ** (k.bit_length() - 1)), (middle, k & -k)):
                source = pieces.get((k ^ mask, at))
                if (k ^ mask) in chips:
                    source = pieces[k ^ mask, 0][:, at : at + middle]
                pieces[k, at] = exchange(source, "group", groups, mask)
    close = [w_own] + [pieces[place] for place in near]
    arrived = swap_rows(own, outgoing)
    close, arrived[1:2], matrix, scale = lax.optimization_barrier((close, arrived[1:2], matrix, scale))
    distant = [place for place in pieces if place not in near]
    last, arrived[2:] = lax.optimization_barrier(([pieces[place] for place in distant], arrived[2:]))
    pieces.update(zip([(0, 0)] + near + distant, close + last))
    for (k, at), piece in list(pieces.items()):
        pieces[k ^ 1, at] = exchange(piece, "group", groups, 1)
    places = sorted(pieces)
    shards = [pieces[place] for place in places]

    half = groups // 2 * shard
    early_width = 3 * width - 128
    x, cot, z, inv_scale, xt = pl.pallas_call(
        norm_kernel,
        out_shape=[
            spec((rows, width), F32),
            spec((rows, width)),
            spec((rows, width), F32),
            spec((rows, 1), F32),
            spec((width, rows)),
        ],
        in_specs=[VMEM] * (1 + n_rows),
        out_specs=[VMEM] * 5,
        compiler_params=limit,
        name="norm",
    )(matrix, *arrived)
    keep, give, out, full, act, slope, bend, g_mixed, g_early = pl.pallas_call(
        partial(forward_kernel, groups, chips, places),
        out_shape=[
            spec((half, early_width)),
            spec((half, early_width)),
            spec((rows, width)),
            spec((width, columns)),
            spec((rows, 4 * width)),
            spec((rows, 4 * width), F32),
            spec((HEADS, rows, rows), F32),
            spec((rows, width)),
            spec((rows, 2 * width)),
        ],
        in_specs=[VMEM] * (5 + len(shards)),
        out_specs=[VMEM] * 9,
        scratch_shapes=[
            pltpu.VMEM((HEADS * rows, rows), BF16),
            pltpu.VMEM((width, rows), BF16),
            pltpu.VMEM((rows, width), F32),
            pltpu.VMEM((rows, width), BF16),
        ],
        compiler_params=limit,
        name="forward",
    )(scale, x, cot, z, xt, *shards)
    taken = exchange(give, "group", groups, 1)
    keep_late, give_late, g_proj = pl.pallas_call(
        partial(backward_kernel, groups, chips[::-1]),
        out_shape=[spec((half, columns - early_width))] * 2 + [spec((rows, 4 * width))],
        in_specs=[VMEM] * 6,
        out_specs=[VMEM] * 3,
        compiler_params=limit,
        name="backward",
    )(xt, act, slope, bend, g_mixed, g_early)
    far = [2**j for j in range(parts.bit_length() - 1)]

    def add(mine, other):
        return mine.astype(F32) + other.astype(F32)

    def both_cores(mine, other, beside):
        return lax.optimization_barrier((add(mine, other).astype(BF16), beside))

    def over_chips(total, masks, beside=()):
        for n, mask in enumerate(masks):
            middle = total.shape[0] // 2
            other = exchange(total[middle:], "group", groups, mask)
            if n == 0:
                other, beside = lax.optimization_barrier((other, beside))
            total = add(total[:middle], other).astype(BF16)
        return total, beside

    side = lax.axis_index("shuf") & 1

    def over_shuf(total):
        middle = shard // 2
        kept = lax.dynamic_slice_in_dim(total, side * middle, middle)
        sent = lax.dynamic_slice_in_dim(total, (1 - side) * middle, middle)
        total = add(kept, exchange(sent, "shuf", parts, 1)).astype(BF16)
        for mask in far[1:]:
            total = add(total, exchange(total, "shuf", parts, mask)).astype(BF16)
        return total, exchange(total, "shuf", parts, 1)

    taken, give_late = lax.optimization_barrier((taken, give_late))
    taken_late = exchange(give_late, "group", groups, 1)
    early, g_proj = both_cores(keep, taken, g_proj)
    returning = pl.pallas_call(
        rows_kernel,
        out_shape=[rows_shape] * n_rows,
        in_specs=[VMEM] * 7,
        out_specs=[VMEM] * n_rows,
        compiler_params=limit,
        name="rows",
    )(matrix, g_proj, full, out, z, inv_scale, cot)
    late, returning = both_cores(keep_late, taken_late, returning)
    returned = swap_rows(returning[0], returning[1:])
    early, returned[1:2] = over_chips(early, chips, returned[1:2])
    owner = pl.pallas_call(
        partial(post_kernel, parts),
        out_shape=[spec((rows, width))] * 2,
        in_specs=[VMEM] * (1 + n_rows),
        out_specs=[VMEM] * 2,
        compiler_params=limit,
        name="post",
    )(send_order, *returned)
    owner_out, owner_grad = owner
    early, owner_out, owner_grad = lax.optimization_barrier((over_shuf(early), owner_out, owner_grad))
    late, _ = over_chips(late, chips[::-1])
    late = over_shuf(late)
    grad_uvqk, grad_wout = pl.pallas_call(
        finish_kernel,
        out_shape=[spec((shard, 4 * width), F32), spec((shard, width), F32)],
        in_specs=[VMEM] * 4,
        out_specs=[HBM] * 2,
        scratch_shapes=[
            pltpu.VMEM((2, shard // 2, 4 * width), F32),
            pltpu.VMEM((2, shard // 2, width), F32),
            pltpu.SemaphoreType.DMA((2, 2)),
        ],
        compiler_params=limit,
        name="finish",
    )(*early, *late)
    return (owner_out[None], owner_grad[None], grad_uvqk, grad_wout)


def solution(mesh):
    data, weight = P("group", "shuf", None), P("group", None)
    return jax.shard_map(
        partial(on_device, mesh.shape["group"], mesh.shape["shuf"]),
        mesh=mesh,
        in_specs=(data, data, weight, weight, data, data, data, data),
        out_specs=(data, data, weight, weight),
        check_vma=False,
    )
```
